512 devices in a mesh: dp: 128 (over y, z, core), mp: 4 (over x).
Axes of the slice: x: 4, y: 4, z: 16, core: 2. Of those that a mesh axis runs over, the one named last changes fastest.
Arguments:
- train_grads: bfloat16 [512, 64, 14336], P('dp', None, 'mp'), may hold values from -6 to 6
- train_acts: bfloat16 [512, 64, 4096], P('dp', None, 'mp'), may hold values from -6 to 6
- query_grads: bfloat16 [128, 64, 14336], P('dp', None, 'mp'), may hold values from -6 to 6
- query_acts: bfloat16 [128, 64, 4096], P('dp', None, 'mp'), may hold values from -6 to 6
- out_factor: bfloat16 [64, 14336], P(None, 'mp'), may hold values from -0.046875 to 0.046875
- in_factor: bfloat16 [64, 4096], P(None, 'mp'), may hold values from -0.09375 to 0.09375
- train_lengths: int32 [512], P('dp'), may hold values from 16 to 64
- query_lengths: int32 [128], P('dp'), may hold values from 16 to 64
Outputs:
- scores: float32 [512, 128], P('dp', 'mp')
The draws below stay inside these ranges and needn't reach their ends.
Inputs may be any that keep to these rules, and one draw needn't show every extreme that they name: `train_lengths`: the number of real tokens of each training example; they are its first positions. `query_lengths`: the number of real tokens of each query example; they are its first positions.
All inputs are finite; a program needn't handle non-finite values.
Results may differ from the reference program's by a relative error of at most 0.0003.
Values sent between devices are 32-bit elements; how exact they have to be, the bound alone decides.
No kernel may reach another device: no remote copies, remote signals or barrier semaphores. Data moves between devices by JAX's collectives and lax.ppermute only.
A program may use at most 128 MiB of HBM per device.

```python
import jax
import jax.numpy as jnp
from jax import lax

D = 4096
FF = 14336
R_OUT = 64
R_IN = 64
SEQ = 64
N_TRAIN = 512
N_QUERY = 128


def place_ends(values, stream_key, least, high):
    index_at = [jax.random.randint(jax.random.fold_in(stream_key, axis), (), 0, length) for axis, length in enumerate(values.shape)]
    longest = values.shape.index(max(values.shape))
    neighbour = index_at[:longest] + [(index_at[longest] + 1) % values.shape[longest]] + index_at[longest + 1:]
    return values.at[tuple(index_at)].set(least).at[tuple(neighbour)].set(high)


def shard_levels(rng, shape, shards, low, largest):
    def one(axis_at, parts):
        steps = jax.random.uniform(jax.random.fold_in(jax.random.fold_in(rng, 6), axis_at), (parts,), jnp.float32, low / len(shards), largest / len(shards))
        return jnp.repeat(jnp.exp(steps), shape[axis_at] // parts).reshape((-1,) + (1,) * (len(shape) - axis_at - 1))

    level = one(*shards[0])
    for cut in shards[1:]:
        level = level * one(*cut)
    return level


def centred(own_key, shape, spread, bound, shards=(), held_as=jnp.bfloat16):
    values = jax.random.normal(own_key, shape, jnp.float32) * spread
    if len(shards) > 0:
        values = shard_levels(own_key, shape, shards, -0.22, 0.18) * values
    return jnp.clip(values, min=-bound, max=bound).astype(held_as)


def setup_inputs(seed: int = 0) -> dict:
    key_of = jax.random.split(jax.random.key(seed), 9)
    return {
        "train_grads": centred(key_of[0], (N_TRAIN, SEQ, FF), 1.0, 6.0, ((0, 128), (2, 4))),
        "train_acts": centred(key_of[1], (N_TRAIN, SEQ, D), 1.0, 6.0, ((0, 128), (2, 4))),
        "query_grads": centred(key_of[2], (N_QUERY, SEQ, FF), 1.0, 6.0, ((0, 128), (2, 4))),
        "query_acts": centred(key_of[3], (N_QUERY, SEQ, D), 1.0, 6.0, ((0, 128), (2, 4))),
        "out_factor": centred(key_of[4], (R_OUT, FF), FF ** -0.5, 0.046875, ((1, 4),)),
        "in_factor": centred(key_of[5], (R_IN, D), D ** -0.5, 0.09375, ((1, 4),)),
        "train_lengths": place_ends(jax.random.randint(key_of[6], (N_TRAIN,), SEQ // 4, SEQ + 1), jax.random.fold_in(key_of[6], 1), SEQ // 4, SEQ).astype(jnp.int32),
        "query_lengths": place_ends(jax.random.randint(key_of[7], (N_QUERY,), SEQ // 4, SEQ + 1), jax.random.fold_in(key_of[7], 1), SEQ // 4, SEQ).astype(jnp.int32),
    }


damping = 2.0

def sketch_rows(grads, activations, lengths, out_factor, in_factor, average):
    examples = grads.shape[0]
    positions = grads.shape[1]
    projected_out = jnp.dot(grads.reshape(examples * positions, grads.shape[2]).astype(jnp.float32), out_factor.T.astype(jnp.float32), preferred_element_type=jnp.float32)
    projected_in = jnp.dot(activations.reshape(examples * positions, activations.shape[2]).astype(jnp.float32), in_factor.T.astype(jnp.float32), preferred_element_type=jnp.float32)
    position = jnp.arange(positions, dtype=jnp.int32)
    weights = (position[None, :] < lengths[:, None]).astype(jnp.float32)
    if average:
        weights = weights / lengths[:, None].astype(jnp.float32)
    weighted = projected_out.reshape(examples, positions, -1) * weights[:, :, None]
    sketch = jnp.einsum('eti,etj->eij', weighted, projected_in.reshape(examples, positions, -1), precision=lax.Precision.HIGHEST)
    return sketch.reshape(examples, -1)

def reference(train_grads, train_acts, query_grads, query_acts, out_factor, in_factor, train_lengths, query_lengths):
    train_sketch = sketch_rows(train_grads, train_acts, train_lengths, out_factor, in_factor, True)
    query_sketch = sketch_rows(query_grads, query_acts, query_lengths, out_factor, in_factor, False)
    gram = jnp.dot(train_sketch.astype(jnp.float32), train_sketch.T.astype(jnp.float32), precision=lax.Precision.HIGHEST, preferred_element_type=jnp.float32)
    cross = jnp.dot(train_sketch.astype(jnp.float32), query_sketch.T.astype(jnp.float32), precision=lax.Precision.HIGHEST, preferred_element_type=jnp.float32)
    damped = gram + damping * jnp.eye(gram.shape[0], dtype=jnp.float32)
    factor = jnp.linalg.cholesky(damped)
    return jax.scipy.linalg.cho_solve((factor, True), cross)
```

```python
import jax
import jax.numpy as jnp
from jax import lax
from jax.experimental import pallas as pl
from jax.experimental.pallas import tpu as pltpu
from jax.sharding import PartitionSpec as P

damping = 2.0
F32 = jnp.float32
HIGHEST = lax.Precision.HIGHEST
VMEM_LIMIT = 40 * 1024 * 1024

NY, NZ, NC = 4, 16, 2
VM = pl.BlockSpec(memory_space=pltpu.VMEM)
SM = pl.BlockSpec(memory_space=pltpu.SMEM)


def params():
    return pltpu.CompilerParams(vmem_limit_bytes=VMEM_LIMIT)


def dot(a, b, ca, cb, precision=HIGHEST):
    return lax.dot_general(
        a, b, (((ca,), (cb,)), ((), ())), precision=precision, preferred_element_type=F32
    )


def project_kernel(tg, ta, qg, qa, of, inf, out):
    n = tg.shape[0] * tg.shape[1]
    out[0:n, 0:64] = dot(tg[...].reshape(n, tg.shape[2]), of[...], 1, 1, None)
    out[0:n, 64:128] = dot(ta[...].reshape(n, ta.shape[2]), inf[...], 1, 1, None)
    m = n + qg.shape[1]
    out[n:m, 0:64] = dot(qg[0], of[...], 1, 1, None)
    out[n:m, 64:128] = dot(qa[0], inf[...], 1, 1, None)


def project(tg, ta, qg, qa, of, inf):
    return pl.pallas_call(
        project_kernel,
        out_shape=jax.ShapeDtypeStruct((320, 128), F32),
        in_specs=[VM] * 6,
        out_specs=VM,
        compiler_params=params(),
        name="project",
    )(tg, ta, qg, qa, of, inf)


def sketch_kernel(pos, tlen, qlen, p0, p1, p2, p3, train, both, sums, square):
    sums[...] = (p0[...] + p1[...]) + (p2[...] + p3[...])
    row = pl.multiple_of(pos[0] * 16, 16)
    token = lax.broadcasted_iota(jnp.int32, (64, 128), 0)
    lane = lax.broadcasted_iota(jnp.int32, (8, 128), 1)
    for e in range(5):
        length = tlen[e] if e < 4 else qlen[0]
        real = (token < length).astype(F32)
        if e < 4:
            real = real / jnp.full((64, 128), length, jnp.int32).astype(F32)
        x = sums[64 * e : 64 * e + 64, :]
        square[...] = dot(x * real, x, 0, 0)
        low = square[pl.ds(row, 8), :]
        high = square[pl.ds(row + 8, 8), :]
        tile = jnp.where(lane < 64, pltpu.roll(low, 64, 1), high)
        if e < 4:
            train[8 * e : 8 * e + 8, :] = tile
        both[8 * e : 8 * e + 8, :] = tile


def sketch(pos, tlen, qlen, parts):
    return pl.pallas_call(
        sketch_kernel,
        out_shape=(
            jax.ShapeDtypeStruct((32, 128), F32),
            jax.ShapeDtypeStruct((40, 128), F32),
        ),
        in_specs=[SM] * 3 + [VM] * 4,
        out_specs=(VM, VM),
        scratch_shapes=[pltpu.VMEM((320, 128), F32), pltpu.VMEM((128, 128), F32)],
        compiler_params=params(),
        name="sketch",
    )(pos, tlen, qlen, *parts)


def tile_kernel(pos, *refs):
    line = refs[:NZ]
    plane = refs[NZ : NZ + 8]
    out, rows, cols = refs[NZ + 8 :]
    y, z, c = pos[1], pos[2], pos[3]
    for t in range(NZ):
        at = lax.rem(z + t, NZ)
        for i in range(4):
            start = pl.multiple_of((i * NZ + at) * 8, 8)
            rows[pl.ds(start, 8), :] = line[t][8 * i : 8 * i + 8, :]
    for h in range(2):
        cols[(24 * h + 20) * 8 : (24 * h + 24) * 8, :] = jnp.zeros((32, 128), F32)
    for t in range(8):
        oy = lax.rem(y + t // 2, NY)
        oc = lax.rem(c + t % 2, NC)
        b = oy * 2 + oc
        start = pl.multiple_of(((b // 4) * 24 + lax.rem(b, 4) * 4) * 8, 8)
        cols[pl.ds(start, 32), :] = plane[t][0:32, :]
        start = pl.multiple_of((oc * 24 + 16 + oy) * 8, 8)
        cols[pl.ds(start, 8), :] = plane[t][32:40, :]
    total = jnp.zeros((48, 64), F32)
    for s in range(8):
        total += dot(cols[pl.ds(s, 48, stride=8), :], rows[pl.ds(s, 64, stride=8), :], 1, 1)
    out[:, 0:64] = total[0:24]
    out[:, 64:128] = total[24:48]


def tile(pos, line, plane):
    return pl.pallas_call(
        tile_kernel,
        out_shape=jax.ShapeDtypeStruct((24, 128), F32),
        in_specs=[SM] + [VM] * (NZ + 8),
        out_specs=VM,
        scratch_shapes=[pltpu.VMEM((512, 128), F32), pltpu.VMEM((384, 128), F32)],
        compiler_params=params(),
        name="tile",
    )(pos, *line, *plane)


def add_kernel(pos, p0, p1, p2, p3, out, sums):
    sums[...] = (p0[...] + p1[...]) + (p2[...] + p3[...])
    out[0:16, :] = sums[0:16, :]
    own = lax.broadcasted_iota(jnp.int32, (8, 128), 0) == pos[0]
    query = jnp.sum(jnp.where(own, sums[16:24, :], 0.0), axis=0, keepdims=True)
    out[16:24, :] = jnp.broadcast_to(query, (8, 128))


def add(pos, parts):
    return pl.pallas_call(
        add_kernel,
        out_shape=jax.ShapeDtypeStruct((24, 128), F32),
        in_specs=[SM] + [VM] * 4,
        out_specs=VM,
        scratch_shapes=[pltpu.VMEM((24, 128), F32)],
        compiler_params=params(),
        name="add",
    )(pos, *parts)


def panel_kernel(pos, *refs):
    parts = refs[:NZ]
    out, held = refs[NZ:]
    for t in range(NZ):
        held[lax.rem(pos[2] + t, NZ)] = parts[t][...]
    for z in range(NZ):
        out[pl.ds(z, 16, stride=NZ), :] = held[z, 0:16, :]
        out[256 + z : 257 + z, :] = held[z, 16:17, :]


def panel(pos, parts):
    return pl.pallas_call(
        panel_kernel,
        out_shape=jax.ShapeDtypeStruct((272, 128), F32),
        in_specs=[SM] + [VM] * NZ,
        out_specs=VM,
        scratch_shapes=[pltpu.VMEM((NZ, 24, 128), F32)],
        compiler_params=params(),
        name="panel",
    )(pos, *parts)


def inverse_factor(tiles):
    lane = lax.broadcasted_iota(jnp.int32, (8, 128), 1)
    count = len(tiles)
    tiles = list(tiles)
    for q in range(count):
        first = 8 * q
        block = tiles[q]
        a = {}
        for c in range(8):
            for p in range(c, 8):
                one = block[p : p + 1, first + c : first + c + 1]
                a[p, c] = jnp.broadcast_to(one, (8, 128))
        w = {}
        low = {}
        for p in range(8):
            scale = lax.rsqrt(a[p, p])
            for k in range(p + 1, 8):
                low[k, p] = a[k, p] * scale
            for k in range(p + 1, 8):
                for c in range(p + 1, k + 1):
                    a[k, c] = a[k, c] - low[k, p] * low[c, p]
            w[p, p] = scale
            for c in range(p):
                part = low[p, c] * w[c, c]
                for k in range(c + 1, p):
                    part = part + low[p, k] * w[k, c]
                w[p, c] = -(part * scale)
        inside = (lane >= first) & (lane < first + 8)
        raw = []
        for c in range(8):
            line = jnp.broadcast_to(block[c : c + 1, :], (8, 128))
            unit = (lane == first + c).astype(F32)
            raw.append(jnp.where(inside, unit, line))
        lines = []
        for p in range(8):
            line = w[p, 0] * raw[0]
            for c in range(1, p + 1):
                line = line + w[p, c] * raw[c]
            lines.append(line)
        sub = lax.broadcasted_iota(jnp.int32, (8, 128), 0)
        merged = lines[0]
        for p in range(1, 8):
            merged = jnp.where(sub == p, lines[p], merged)
        tiles[q] = merged
        for r in range(q + 1, count):
            cols = [
                jnp.broadcast_to(tiles[r][:, first + c : first + c + 1], (8, 128))
                for c in range(8)
            ]
            update = None
            for p in range(8):
                part = w[p, 0] * cols[0]
                for c in range(1, p + 1):
                    part = part + w[p, c] * cols[c]
                update = part * lines[p] if update is None else update + part * lines[p]
            tiles[r] = jnp.where(inside, 0.0, tiles[r]) - update
    for q in range(count):
        row = lax.broadcasted_iota(jnp.int32, (8, 128), 0) + 8 * q
        tiles[q] = jnp.where(lane <= row, tiles[q], 0.0)
    return tiles


def solve_kernel(pos, *refs):
    panels = refs[:8]
    out, order, full, inv, x = refs[8:]
    m, y, z, c = pos[0], pos[1], pos[2], pos[3]
    lane = lax.broadcasted_iota(jnp.int32, (256, 128), 1)
    left = lane < 64
    for t in range(8):
        b = lax.rem(y + t // 2, NY) * 2 + lax.rem(c + t % 2, NC)
        order[b] = panels[t][...]
    for j in range(NY):
        even = order[2 * j, 0:256, :]
        odd = order[2 * j + 1, 0:256, :]
        full[0:256, 128 * j : 128 * j + 128] = jnp.where(left, even, pltpu.roll(odd, 64, 1))
        full[256:512, 128 * j : 128 * j + 128] = jnp.where(left, pltpu.roll(even, 64, 1), odd)
    for b in range(8):
        both = order[b, 256:272, :]
        stacked = jnp.concatenate([both, both, both, both, both, both, both, both], axis=0)
        turned = stacked.T
        lane1 = lax.broadcasted_iota(jnp.int32, (64, 128), 1)
        pick = jnp.where(lane1 < 16, turned[0:64, :], turned[64:128, :])
        full[64 * b : 64 * b + 64, 512:640] = jnp.where(lane1 < 32, pick, 0.0)
    eye = (
        lax.broadcasted_iota(jnp.int32, (128, 128), 0)
        == lax.broadcasted_iota(jnp.int32, (128, 128), 1)
    ).astype(F32) * damping
    for k in range(4):
        s = slice(128 * k, 128 * k + 128)
        full[s, s] = full[s, s] + eye

    def step(k, carry):
        at = pl.multiple_of(k * 128, 128)
        tiles = [full[pl.ds(at + 8 * t, 8), pl.ds(at, 128)] for t in range(16)]
        tiles = inverse_factor(tiles)
        for t in range(16):
            inv[k, 8 * t : 8 * t + 8, :] = tiles[t]
        strip = dot(inv[k], full[pl.ds(at, 128), :], 1, 0)
        full[pl.ds(at, 128), :] = strip

        def trail(i, inner):
            to = pl.multiple_of(i * 128, 128)
            mine = full[pl.ds(at, 128), pl.ds(to, 128)]
            full[pl.ds(to, 128), :] -= dot(mine, full[pl.ds(at, 128), :], 0, 0)
            return inner

        return lax.fori_loop(k + 1, 4, trail, carry)

    lax.fori_loop(0, 4, step, 0)
    for k in (3, 2, 1, 0):
        s = slice(128 * k, 128 * k + 128)
        rest = full[s, 512:640]
        if k < 3:
            rest = rest - dot(full[s, 128 * k + 128 : 512], x[128 * k + 128 : 512, :], 1, 0)
        x[s, :] = dot(inv[k], rest, 0, 0)
    sub = lax.broadcasted_iota(jnp.int32, (8, 128), 0)
    for i in range(4):
        start = pl.multiple_of((y * 2 + c) * 64 + i * 16 + (z // 8) * 8, 8)
        eight = x[pl.ds(start, 8), :]
        one = jnp.sum(jnp.where(sub == lax.rem(z, 8), eight, 0.0), axis=0, keepdims=True)
        out[i : i + 1, :] = one


def solve(pos, panels):
    return pl.pallas_call(
        solve_kernel,
        out_shape=jax.ShapeDtypeStruct((4, 128), F32),
        in_specs=[SM] + [VM] * 8,
        out_specs=VM,
        scratch_shapes=[
            pltpu.VMEM((8, 272, 128), F32),
            pltpu.VMEM((512, 640), F32),
            pltpu.VMEM((4, 128, 128), F32),
            pltpu.VMEM((512, 128), F32),
        ],
        compiler_params=params(),
        name="solve",
    )(pos, *panels)


def index(y, z, c):
    return ((y % NY) * NZ + z % NZ) * NC + c % NC


def from_dp(value, dy, dz, dc):
    pairs = [
        (index(y + dy, z + dz, c + dc), index(y, z, c))
        for y in range(NY)
        for z in range(NZ)
        for c in range(NC)
    ]
    return lax.ppermute(value, "dp", pairs)


def from_mp(value, dx):
    return lax.ppermute(value, "mp", [((x + dx) % 4, x) for x in range(4)])


def shards(tg, ta, qg, qa, of, inf, tlen, qlen):
    d = lax.axis_index("dp")
    m = lax.axis_index("mp")
    pos = jnp.stack([m, d // (NZ * NC), (d // NC) % NZ, d % NC]).astype(jnp.int32)
    partial = project(tg, ta, qg, qa, of, inf)
    train, both = sketch(pos, tlen, qlen, [partial] + [from_mp(partial, s) for s in (1, 2, 3)])
    copies = jnp.broadcast_to(train[None], (NZ, 32, 128))
    groups = [[index(y, z, c) for z in range(NZ)] for y in range(NY) for c in range(NC)]
    zline = lax.all_to_all(copies, "dp", 0, 0, axis_index_groups=groups, tiled=True)
    z = pos[2]
    line = [zline[s] for s in range(NZ)]
    plane = [both] + [from_dp(both, t // 2, 0, t % 2) for t in range(1, 8)]
    part = tile(jnp.stack([pos[0], pos[1], 0 * z, pos[3]]), line, plane)
    summed = add(pos, [part] + [from_mp(part, s) for s in (1, 2, 3)])
    own = panel(pos, [summed] + [from_dp(summed, 0, s, 0) for s in range(1, NZ)])
    ys = [own] + [from_dp(own, s, 0, 0) for s in (1, 2, 3)]
    panels = []
    for s in range(4):
        panels += [ys[s], from_dp(ys[s], 0, 0, 1)]
    result = solve(pos, panels)[:, :32]
    return result.reshape(4, 2, 16).transpose(0, 2, 1).reshape(4, 32)


def solution(mesh):
    return jax.shard_map(
        shards,
        mesh=mesh,
        in_specs=(
            P("dp", None, "mp"),
            P("dp", None, "mp"),
            P("dp", None, "mp"),
            P("dp", None, "mp"),
            P(None, "mp"),
            P(None, "mp"),
            P("dp"),
            P("dp"),
        ),
        out_specs=P("dp", "mp"),
        check_vma=False,
    )
```

```python
import jax
import jax.numpy as jnp
from jax import lax
from jax.experimental import pallas as pl
from jax.experimental.pallas import tpu as pltpu
from jax.sharding import PartitionSpec as P

damping = 2.0
F32 = jnp.float32
HIGHEST = lax.Precision.HIGHEST
MB = 1024 * 1024

NY, NZ, NC = 4, 16, 2
VM = pl.BlockSpec(memory_space=pltpu.VMEM)
SM = pl.BlockSpec(memory_space=pltpu.SMEM)
ANY = pl.BlockSpec(memory_space=pl.ANY)


def params(limit=40 * MB):
    return pltpu.CompilerParams(vmem_limit_bytes=limit)


def shape(*sizes):
    return jax.ShapeDtypeStruct(sizes, F32)


def dot(a, b, ca, cb, precision=HIGHEST):
    return lax.dot_general(
        a, b, (((ca,), (cb,)), ((), ())), precision=precision, preferred_element_type=F32
    )


def lanes(*sizes):
    return lax.broadcasted_iota(jnp.int32, sizes, 1)


CHUNKS = 4


def project_kernel(tg, ta, qg, qa, of, inf, out, g, a, fo, fi, acc, sem):
    copies = []

    def start(src, dst):
        copy = pltpu.make_async_copy(src, dst, sem.at[len(copies)])
        copy.start()
        copies.append(copy)

    start(inf.at[0:32], fi.at[32:64])
    start(inf.at[32:64], fi.at[96:128])
    start(ta, a.at[0:4])
    start(qa, a.at[4:5])
    start(of.at[0:32], fo.at[0:32])
    start(of.at[32:64], fo.at[64:96])
    width = g.shape[2] // CHUNKS
    for j in range(CHUNKS):
        s = slice(j * width, (j + 1) * width)
        start(tg.at[:, :, s], g.at[0:4, :, s])
        start(qg.at[:, :, s], g.at[4:5, :, s])
    for at in (0, 64):
        fi[at : at + 32, :] = jnp.zeros((32, fi.shape[1]), fi.dtype)
        fo[at + 32 : at + 64, :] = jnp.zeros((32, fo.shape[1]), fo.dtype)
    for copy in copies[:4]:
        copy.wait()
    acc[...] = dot(a[...].reshape(320, a.shape[2]), fi[...], 1, 1, None)
    copies[4].wait()
    copies[5].wait()
    for j in range(CHUNKS):
        copies[6 + 2 * j].wait()
        copies[7 + 2 * j].wait()
        s = slice(j * width, (j + 1) * width)
        acc[...] += dot(g[:, :, s].reshape(320, width), fo[:, s], 1, 1, None)
    for low, high, to, n in ((0, 128, 0, 128), (256, 288, 128, 32)):
        left = lanes(n, 128) < 64
        first = acc[low : low + n, :]
        second = acc[high : high + n, :]
        for p in range(4):
            one = pltpu.roll(first, (128 - 32 * p) % 128, 1) if p else first
            two = pltpu.roll(second, (64 - 32 * p) % 128, 1) if p != 2 else second
            out[p, to : to + n, :] = jnp.where(left, one, two)


def project(tg, ta, qg, qa, of, inf):
    kg, ka = tg.shape[2], ta.shape[2]
    return pl.pallas_call(
        project_kernel,
        out_shape=shape(4, 160, 128),
        in_specs=[ANY] * 6,
        out_specs=VM,
        scratch_shapes=[
            pltpu.VMEM((5, 64, kg), jnp.bfloat16),
            pltpu.VMEM((5, 64, ka), jnp.bfloat16),
            pltpu.VMEM((128, kg), jnp.bfloat16),
            pltpu.VMEM((128, ka), jnp.bfloat16),
            pltpu.VMEM((320, 128), F32),
            pltpu.SemaphoreType.DMA((6 + 2 * CHUNKS,)),
        ],
        compiler_params=params(56 * MB),
        name="project",
    )(tg, ta, qg, qa, of, inf)


def sketch_kernel(tlen, qlen, parts, zcopies, own, square):
    lane = lanes(8, 128)

    def fold(row, col):
        total = None
        for g in range(4):
            piece = square[row + 8 * g : row + 8 * g + 8, :]
            shift = (32 * g - col) % 128
            piece = pltpu.roll(piece, shift, 1) if shift else piece
            piece = jnp.where((lane >= 32 * g) & (lane < 32 * g + 32), piece, 0.0)
            total = piece if total is None else total + piece
        return total

    def emit(e, tile):
        for t in range(NZ):
            if e < 4:
                zcopies[t, 8 * e : 8 * e + 8, :] = tile
        own[8 * e : 8 * e + 8, :] = tile

    def outer(low, n, weight):
        s = slice(low, low + n)
        x = (parts[0, s, :] + parts[1, s, :]) + (parts[2, s, :] + parts[3, s, :])
        square[...] = dot(x * weight, x, 0, 0)

    token = lax.broadcasted_iota(jnp.int32, (64, 128), 0)
    left = lanes(64, 128) < 64
    for e in range(2):
        length = jnp.where(left, tlen[e], tlen[e + 2])
        weight = (token < length).astype(F32) / length.astype(F32)
        outer(64 * e, 64, weight)
        emit(e, fold(0, 32))
        emit(e + 2, fold(64, 96))
    token = token[0:32] + jnp.where(left[0:32], 0, 32)
    outer(128, 32, (token < qlen[0]).astype(F32))
    emit(4, fold(0, 32) + fold(64, 96))


def sketch(tlen, qlen, parts):
    return pl.pallas_call(
        sketch_kernel,
        out_shape=(shape(NZ, 32, 128), shape(40, 128)),
        in_specs=[SM] * 2 + [VM],
        out_specs=(VM, VM),
        scratch_shapes=[pltpu.VMEM((128, 128), F32)],
        compiler_params=params(),
        name="sketch",
    )(tlen, qlen, parts)


def tile_kernel(pos, line, p0, p1, p2, p3, out, cols, held):
    y = pos[0] // (NZ * NC)
    c = lax.rem(pos[0], NC)
    for t, pair in enumerate((p0, p1, p2, p3)):
        for h in range(2):
            b = lax.rem(y + t, NY) * NC + lax.rem(c + h, NC)
            start = pl.multiple_of(b * 40, 8)
            cols[pl.ds(start, 40), :] = pair[40 * h : 40 * h + 40, :]
    total = None
    for s in range(8):
        rows = [line[pl.ds(8 * i + s, NZ, stride=32), :] for i in range(4)]
        part = dot(cols[pl.ds(s, 40, stride=8), :], jnp.concatenate(rows, axis=0), 1, 1)
        total = part if total is None else total + part
    held[:, 0:64] = total
    held[:, 64:128] = total
    for p in range(4):
        out[p] = jnp.zeros((8, 128), F32)
        for h in range(2):
            s = slice(64 * h, 64 * h + 64)
            row = 5 * (4 * h + p)
            out[p, 0:4, s] = held[row : row + 4, s]
            row = 5 * (2 * p + h) + 4
            out[p, 4:5, s] = held[row : row + 1, s]


def tile(pos, line, pairs):
    return pl.pallas_call(
        tile_kernel,
        out_shape=shape(4, 8, 128),
        in_specs=[SM] + [VM] * 5,
        out_specs=VM,
        scratch_shapes=[pltpu.VMEM((320, 128), F32), pltpu.VMEM((40, 128), F32)],
        compiler_params=params(),
        name="tile",
    )(pos, line, *pairs)


def add_kernel(parts, out):
    total = (parts[0] + parts[1]) + (parts[2] + parts[3])
    for t in range(NZ):
        out[t] = total


def add(parts):
    return pl.pallas_call(
        add_kernel,
        out_shape=shape(NZ, 8, 128),
        in_specs=[VM],
        out_specs=VM,
        compiler_params=params(),
        name="add",
    )(parts)


def panel_kernel(parts, out):
    for z in range(NZ):
        gram = parts[z, 0:4, :]
        query = parts[z, 4:5, :]
        for t in range(NY * 4):
            out[t, pl.ds(z, 4, stride=NZ), :] = gram
            out[t, 64 + z : 65 + z, :] = query


def panel(parts):
    return pl.pallas_call(
        panel_kernel,
        out_shape=shape(NY * 4, 80, 128),
        in_specs=[VM],
        out_specs=VM,
        compiler_params=params(),
        name="panel",
    )(parts)


def inverse_factor(tiles):
    lane = lanes(8, 128)
    sub = lax.broadcasted_iota(jnp.int32, (8, 128), 0)
    count = len(tiles)
    tiles = list(tiles)
    for q in range(count):
        first = 8 * q
        block = tiles[q]
        inside = (lane >= first) & (lane < first + 8)

        def column(r, c):
            return jnp.broadcast_to(tiles[r][:, first + c : first + c + 1], (8, 128))

        a = {}
        for c in range(8):
            whole = column(q, c)
            for p in range(c, 8):
                a[p, c] = jnp.broadcast_to(whole[p : p + 1, :], (8, 128))
        low = {}
        scale = []
        lines = []
        for p in range(8):
            scale.append(lax.rsqrt(a[p, p]))
            for k in range(p + 1, 8):
                low[k, p] = a[k, p] * scale[p]
            for k in range(p + 1, 8):
                for c in range(p + 1, k + 1):
                    a[k, c] = a[k, c] - low[k, p] * low[c, p]
            unit = (lane == first + p).astype(F32)
            line = jnp.where(inside, unit, jnp.broadcast_to(block[p : p + 1, :], (8, 128)))
            for k in range(p):
                line = line - low[p, k] * lines[k]
            lines.append(line * scale[p])
        merged = lines[0]
        for p in range(1, 8):
            merged = jnp.where(sub == p, lines[p], merged)
        tiles[q] = merged
        if q + 1 < count:
            rest = jnp.where(inside, 0.0, tiles[q + 1])
            cols = []
            for p in range(8):
                col = column(q + 1, p)
                for k in range(p):
                    col = col - low[p, k] * cols[k]
                cols.append(col * scale[p])
                rest = rest - cols[p] * lines[p]
        if q + 2 < count:
            back = [None] * 8
            for p in range(7, -1, -1):
                line = lines[p]
                for k in range(7, p, -1):
                    line = line - low[k, p] * back[k]
                back[p] = line * scale[p]
            other = jnp.where(inside, 0.0, tiles[q + 2])
            for c in range(8):
                other = other - column(q + 2, c) * back[c]
            tiles[q + 2] = other
        if q + 3 < count:
            stacked = back[0]
            for p in range(1, 8):
                stacked = jnp.where(sub == p, back[p], stacked)
            far = dot(block, stacked, 0, 0)
            for r in range(q + 3, count):
                tiles[r] = jnp.where(inside, 0.0, tiles[r]) - far[8 * r : 8 * r + 8, :]
        if q + 1 < count:
            tiles[q + 1] = rest
    for q in range(count):
        tiles[q] = jnp.where(lane <= sub + 8 * q, tiles[q], 0.0)
    return tiles


def solve_kernel(pos, mine, theirs, out, full, inv, turn):
    d = pos[0]
    y = d // (NZ * NC)
    z = lax.rem(d // NC, NZ)
    c = lax.rem(d, NC)
    base = (y * NC + c) * 64 + z
    first = c == 0
    lane = lanes(128, 128)
    row = lax.broadcasted_iota(jnp.int32, (128, 128), 0)
    left = lane < 64
    eye = (lane == row).astype(F32) * damping

    def split(at, s):
        one, two = mine[at, s, :], theirs[at, s, :]
        return jnp.where(first, one, two), jnp.where(first, two, one)

    for j in range(NY):
        for k in range(j + 1):
            halves = []
            for g in (2 * (k % 2), 2 * (k % 2) + 1):
                even, odd = split(4 * j + g, slice(0, 64))
                if k < 2:
                    halves.append(jnp.where(left[:64], even, pltpu.roll(odd, 64, 1)))
                else:
                    halves.append(jnp.where(left[:64], pltpu.roll(even, 64, 1), odd))
            block = jnp.concatenate(halves, axis=0)
            if j == k:
                block = block + eye
            full[128 * k : 128 * k + 128, 128 * j : 128 * j + 128] = block
        even, odd = split(4 * j + pos[1], slice(64, 80))
        turn[pl.ds(0, 16, stride=2), :] = jnp.where(left[:16], even, pltpu.roll(odd, 64, 1))
        turn[pl.ds(1, 16, stride=2), :] = jnp.where(left[:16], pltpu.roll(even, 64, 1), odd)
        turned = turn[...].T
        unit = (row + 128 * j == base + (lane - 32) * 16).astype(F32)
        right = jnp.where(lane < 32, turned, jnp.where(lane < 36, unit, 0.0))
        full[128 * j : 128 * j + 128, 512:640] = right
    product = None
    diagonal = full[0:128, 0:128]
    for k in range(4):
        s = slice(128 * k, 128 * k + 128)
        tiles = inverse_factor([diagonal[8 * t : 8 * t + 8, :] for t in range(16)])
        for t in range(16):
            inv[k, 8 * t : 8 * t + 8, :] = tiles[t]
        after = 128 * k + 128
        if k < 3:
            n = slice(after, after + 128)
            strip = dot(inv[k], full[s, n], 1, 0)
            full[s, n] = strip
            diagonal = full[n, n] - dot(strip, strip, 0, 0)
            rest = slice(after + 128, 640)
            full[s, rest] = dot(inv[k], full[s, rest], 1, 0)
            full[n, rest] -= dot(full[s, n], full[s, rest], 0, 0)
            for i in range(k + 2, 4):
                to = slice(128 * i, 128 * i + 128)
                full[to, 128 * i : 640] -= dot(full[s, to], full[s, 128 * i : 640], 0, 0)
        else:
            full[s, after:640] = dot(inv[k], full[s, after:640], 1, 0)
        part = dot(full[s, 512:640], full[s, 512:640], 0, 0)
        product = part if product is None else product + part
    out[...] = product[32:36, 0:32]


def solve(pos, mine, theirs):
    return pl.pallas_call(
        solve_kernel,
        out_shape=shape(4, 32),
        in_specs=[SM] + [VM] * 2,
        out_specs=VM,
        scratch_shapes=[
            pltpu.VMEM((512, 640), F32),
            pltpu.VMEM((4, 128, 128), F32),
            pltpu.VMEM((128, 128), F32),
        ],
        compiler_params=params(),
        name="solve",
    )(pos, mine, theirs)


def index(y, z, c):
    return (y * NZ + z) * NC + c


def exchange(value, axes, groups):
    return lax.all_to_all(value, axes, 0, 0, axis_index_groups=groups, tiled=True)


def shards(tg, ta, qg, qa, of, inf, tlen, qlen):
    ys, zs, cs = range(NY), range(NZ), range(NC)
    everyone = [(y, z, c) for y in ys for z in zs for c in cs]
    line_groups = [[index(y, z, c) for z in zs] for y in ys for c in cs]
    face_groups = [
        [index(y, z, c) * 4 + x for y in ys for x in range(4)] for z in zs for c in cs
    ]
    cores = [(index(y, z, 1 - c), index(y, z, c)) for y, z, c in everyone]
    pos = jnp.stack([lax.axis_index("dp"), lax.axis_index("mp")]).astype(jnp.int32)
    parts = project(tg, ta, qg, qa, of, inf)
    parts = lax.all_to_all(parts, "mp", 0, 0, tiled=True)
    zcopies, own = sketch(tlen, qlen, parts)
    line = exchange(zcopies, "dp", line_groups).reshape(NZ * 32, 128)
    pair = jnp.concatenate([own, lax.ppermute(own, "dp", cores)], axis=0)
    pairs = [pair]
    for t in (1, 2, 3):
        from_y = [(index((y + t) % NY, z, c), index(y, z, c)) for y, z, c in everyone]
        pairs.append(lax.ppermute(pair, "dp", from_y))
    tiles = lax.all_to_all(tile(pos, line, pairs), "mp", 0, 0, tiled=True)
    panels = panel(exchange(add(tiles), "dp", line_groups))
    mine = exchange(panels, ("dp", "mp"), face_groups)
    theirs = lax.ppermute(mine, "dp", cores)
    return solve(pos, mine, theirs)


def solution(mesh):
    return jax.shard_map(
        shards,
        mesh=mesh,
        in_specs=(
            P("dp", None, "mp"),
            P("dp", None, "mp"),
            P("dp", None, "mp"),
            P("dp", None, "mp"),
            P(None, "mp"),
            P(None, "mp"),
            P("dp"),
            P("dp"),
        ),
        out_specs=P("dp", "mp"),
        check_vma=False,
    )
```

```python
import jax
import jax.numpy as jnp
from jax import lax
from jax.experimental import pallas as pl
from jax.experimental.pallas import tpu as pltpu
from jax.sharding import PartitionSpec as P

damping = 2.0
F32 = jnp.float32
HIGHEST = lax.Precision.HIGHEST
MB = 1024 * 1024

NY, NZ, NC = 4, 16, 2
VM = pl.BlockSpec(memory_space=pltpu.VMEM)
SM = pl.BlockSpec(memory_space=pltpu.SMEM)
ANY = pl.BlockSpec(memory_space=pl.ANY)


def params(limit=40 * MB):
    return pltpu.CompilerParams(vmem_limit_bytes=limit)


def shape(*sizes):
    return jax.ShapeDtypeStruct(sizes, F32)


def dot(a, b, ca, cb, precision=HIGHEST):
    return lax.dot_general(
        a, b, (((ca,), (cb,)), ((), ())), precision=precision, preferred_element_type=F32
    )


def lanes(*sizes):
    return lax.broadcasted_iota(jnp.int32, sizes, 1)


CHUNKS = 4


def project_kernel(tg, ta, qg, qa, of, inf, out, g, a, fo, fi, acc, sem):
    copies = []

    def start(src, dst):
        copy = pltpu.make_async_copy(src, dst, sem.at[len(copies)])
        copy.start()
        copies.append(copy)

    start(inf.at[0:32], fi.at[32:64])
    start(inf.at[32:64], fi.at[96:128])
    start(ta, a.at[0:4])
    start(qa, a.at[4:5])
    start(of.at[0:32], fo.at[0:32])
    start(of.at[32:64], fo.at[64:96])
    width = g.shape[2] // CHUNKS
    for j in range(CHUNKS):
        s = slice(j * width, (j + 1) * width)
        start(tg.at[:, :, s], g.at[0:4, :, s])
        start(qg.at[:, :, s], g.at[4:5, :, s])
    for at in (0, 64):
        fi[at : at + 32, :] = jnp.zeros((32, fi.shape[1]), fi.dtype)
        fo[at + 32 : at + 64, :] = jnp.zeros((32, fo.shape[1]), fo.dtype)
    for copy in copies[:4]:
        copy.wait()
    acc[...] = dot(a[...].reshape(320, a.shape[2]), fi[...], 1, 1, None)
    copies[4].wait()
    copies[5].wait()
    for j in range(CHUNKS):
        copies[6 + 2 * j].wait()
        copies[7 + 2 * j].wait()
        s = slice(j * width, (j + 1) * width)
        acc[...] += dot(g[:, :, s].reshape(320, width), fo[:, s], 1, 1, None)
    for low, high, to, n in ((0, 128, 0, 128), (256, 288, 128, 32)):
        left = lanes(n, 128) < 64
        first = acc[low : low + n, :]
        second = acc[high : high + n, :]
        for p in range(4):
            one = pltpu.roll(first, (128 - 32 * p) % 128, 1) if p else first
            two = pltpu.roll(second, (64 - 32 * p) % 128, 1) if p != 2 else second
            out[p, to : to + n, :] = jnp.where(left, one, two)


def project(tg, ta, qg, qa, of, inf):
    kg, ka = tg.shape[2], ta.shape[2]
    return pl.pallas_call(
        project_kernel,
        out_shape=shape(4, 160, 128),
        in_specs=[ANY] * 6,
        out_specs=VM,
        scratch_shapes=[
            pltpu.VMEM((5, 64, kg), jnp.bfloat16),
            pltpu.VMEM((5, 64, ka), jnp.bfloat16),
            pltpu.VMEM((128, kg), jnp.bfloat16),
            pltpu.VMEM((128, ka), jnp.bfloat16),
            pltpu.VMEM((320, 128), F32),
            pltpu.SemaphoreType.DMA((6 + 2 * CHUNKS,)),
        ],
        compiler_params=params(56 * MB),
        name="project",
    )(tg, ta, qg, qa, of, inf)


def sketch_kernel(tlen, qlen, parts, zcopies, own, square):
    lane = lanes(8, 128)

    def fold(row, col):
        total = None
        for g in range(4):
            piece = square[row + 8 * g : row + 8 * g + 8, :]
            shift = (32 * g - col) % 128
            piece = pltpu.roll(piece, shift, 1) if shift else piece
            piece = jnp.where((lane >= 32 * g) & (lane < 32 * g + 32), piece, 0.0)
            total = piece if total is None else total + piece
        return total

    def emit(e, tile):
        for t in range(NZ):
            if e < 4:
                zcopies[t, 8 * e : 8 * e + 8, :] = tile
        own[8 * e : 8 * e + 8, :] = tile

    def outer(low, n, weight):
        s = slice(low, low + n)
        x = (parts[0, s, :] + parts[1, s, :]) + (parts[2, s, :] + parts[3, s, :])
        square[...] = dot(x * weight, x, 0, 0)

    token = lax.broadcasted_iota(jnp.int32, (64, 128), 0)
    left = lanes(64, 128) < 64
    for e in range(2):
        length = jnp.where(left, tlen[e], tlen[e + 2])
        weight = (token < length).astype(F32) / length.astype(F32)
        outer(64 * e, 64, weight)
        emit(e, fold(0, 32))
        emit(e + 2, fold(64, 96))
    token = token[0:32] + jnp.where(left[0:32], 0, 32)
    outer(128, 32, (token < qlen[0]).astype(F32))
    emit(4, fold(0, 32) + fold(64, 96))


def sketch(tlen, qlen, parts):
    return pl.pallas_call(
        sketch_kernel,
        out_shape=(shape(NZ, 32, 128), shape(40, 128)),
        in_specs=[SM] * 2 + [VM],
        out_specs=(VM, VM),
        scratch_shapes=[pltpu.VMEM((128, 128), F32)],
        compiler_params=params(),
        name="sketch",
    )(tlen, qlen, parts)


def tile_kernel(pos, line, near, away, out, cols, held):
    y = pos[0] // (NZ * NC)
    c = lax.rem(pos[0], NC)
    for t, pairs in enumerate((near, near, away, away)):
        at = y if t < 2 else NY - 1 - y
        at = at if t % 2 == 0 else at + 1 - 2 * lax.rem(at, 2)
        for h in range(2):
            b = at * NC + lax.rem(c + h, NC)
            start = pl.multiple_of(b * 40, 8)
            row = 80 * (t % 2) + 40 * h
            cols[pl.ds(start, 40), :] = pairs[row : row + 40, :]
    total = None
    for s in range(8):
        rows = [line[pl.ds(8 * i + s, NZ, stride=32), :] for i in range(4)]
        part = dot(cols[pl.ds(s, 40, stride=8), :], jnp.concatenate(rows, axis=0), 1, 1)
        total = part if total is None else total + part
    held[:, 0:64] = total
    held[:, 64:128] = total
    for p in range(4):
        out[p, 16:24, :] = jnp.zeros((8, 128), F32)
        for h in range(2):
            s = slice(64 * h, 64 * h + 64)
            for g in range(4):
                row = 5 * (4 * h + g)
                out[p, 4 * g : 4 * g + 4, s] = held[row : row + 4, s]
            row = 5 * (2 * p + h) + 4
            out[p, 16:17, s] = held[row : row + 1, s]


def tile(pos, line, near, away):
    return pl.pallas_call(
        tile_kernel,
        out_shape=shape(4, 24, 128),
        in_specs=[SM] + [VM] * 3,
        out_specs=VM,
        scratch_shapes=[pltpu.VMEM((320, 128), F32), pltpu.VMEM((40, 128), F32)],
        compiler_params=params(),
        name="tile",
    )(pos, line, near, away)


def add_kernel(parts, out):
    total = (parts[0] + parts[1]) + (parts[2] + parts[3])
    for t in range(NZ):
        out[t] = total


def add(parts):
    return pl.pallas_call(
        add_kernel,
        out_shape=shape(NZ, 24, 128),
        in_specs=[VM],
        out_specs=VM,
        compiler_params=params(),
        name="add",
    )(parts)


def panel_kernel(parts, out):
    for z in range(NZ):
        both = parts[z, 0:16, :]
        query = parts[z, 16:17, :]
        for t in range(NY):
            out[t, pl.ds(z, 16, stride=NZ), :] = both
            out[t, 256 + z : 257 + z, :] = query


def panel(parts):
    return pl.pallas_call(
        panel_kernel,
        out_shape=shape(NY, 272, 128),
        in_specs=[VM],
        out_specs=VM,
        compiler_params=params(),
        name="panel",
    )(parts)


def inverse_factor(tiles):
    lane = lanes(8, 128)
    sub = lax.broadcasted_iota(jnp.int32, (8, 128), 0)
    count = len(tiles)
    tiles = list(tiles)
    for q in range(count):
        first = 8 * q
        block = tiles[q]
        inside = (lane >= first) & (lane < first + 8)

        def column(r, c):
            return jnp.broadcast_to(tiles[r][:, first + c : first + c + 1], (8, 128))

        a = {}
        for c in range(8):
            whole = column(q, c)
            for p in range(c, 8):
                a[p, c] = jnp.broadcast_to(whole[p : p + 1, :], (8, 128))
        mult = {}
        lines, scaled, rows = [], [], []
        for p in range(0, 8, 2):
            d, o, e = a[p, p], a[p + 1, p], a[p + 1, p + 1]
            root = lax.rsqrt(d * e - o * o)
            inverse = root * root
            for k in range(p + 2, 8):
                mult[k, p] = (a[k, p] * e - a[k, p + 1] * o) * inverse
                mult[k, p + 1] = (a[k, p + 1] * d - a[k, p] * o) * inverse
            for k in range(p + 2, 8):
                for c in range(p + 2, k + 1):
                    a[k, c] = a[k, c] - (mult[k, p] * a[c, p] + mult[k, p + 1] * a[c, p + 1])
            for r in (p, p + 1):
                unit = (lane == first + r).astype(F32)
                line = jnp.broadcast_to(block[r : r + 1, :], (8, 128))
                line = jnp.where(inside, unit, line)
                for k in range(p):
                    line = line - mult[r, k] * lines[k]
                lines.append(line)
            low, high = lines[p], lines[p + 1]
            turned = high * d - low * o
            scaled.append((low * e - high * o) * inverse)
            scaled.append(turned * inverse)
            top = lax.rsqrt(d)
            rows.append(low * top)
            rows.append(turned * (top * root))
        merged = rows[0]
        for p in range(1, 8):
            merged = jnp.where(sub == p, rows[p], merged)
        tiles[q] = merged
        if q + 1 < count:
            rest = jnp.where(inside, 0.0, tiles[q + 1])
            cols = []
            for p in range(0, 8, 2):
                for r in (p, p + 1):
                    col = column(q + 1, r)
                    for k in range(p):
                        col = col - mult[r, k] * cols[k]
                    cols.append(col)
                rest = rest - (cols[p] * scaled[p] + cols[p + 1] * scaled[p + 1])
        if q + 2 < count:
            back = list(scaled)
            for p in range(5, -1, -1):
                for k in range(7, p + 1 - p % 2, -1):
                    back[p] = back[p] - mult[k, p] * back[k]
            other = jnp.where(inside, 0.0, tiles[q + 2])
            for c in range(8):
                other = other - column(q + 2, c) * back[c]
            tiles[q + 2] = other
        if q + 3 < count:
            stacked = back[0]
            for p in range(1, 8):
                stacked = jnp.where(sub == p, back[p], stacked)
            far = dot(block, stacked, 0, 0)
            for r in range(q + 3, count):
                tiles[r] = jnp.where(inside, 0.0, tiles[r]) - far[8 * r : 8 * r + 8, :]
        if q + 1 < count:
            tiles[q + 1] = rest
    for q in range(count):
        tiles[q] = jnp.where(lane <= sub + 8 * q, tiles[q], 0.0)
    return tiles


def solve_kernel(pos, mine, theirs, out, full, inv, turn):
    d = pos[0]
    y = d // (NZ * NC)
    z = lax.rem(d // NC, NZ)
    c = lax.rem(d, NC)
    base = (y * NC + c) * 64 + z
    first = c == 0
    lane = lanes(128, 128)
    row = lax.broadcasted_iota(jnp.int32, (128, 128), 0)
    left = lane < 64
    eye = (lane == row).astype(F32) * damping

    for j in range(NY):
        for k in range(j + 1):
            s = slice(128 * (k % 2), 128 * (k % 2) + 128)
            even = jnp.where(first, mine[j, s, :], theirs[j, s, :])
            odd = jnp.where(first, theirs[j, s, :], mine[j, s, :])
            if k < 2:
                block = jnp.where(left, even, pltpu.roll(odd, 64, 1))
            else:
                block = jnp.where(left, pltpu.roll(even, 64, 1), odd)
            if j == k:
                block = block + eye
            full[128 * k : 128 * k + 128, 128 * j : 128 * j + 128] = block
        even = jnp.where(first, mine[j, 256:272, :], theirs[j, 256:272, :])
        odd = jnp.where(first, theirs[j, 256:272, :], mine[j, 256:272, :])
        turn[pl.ds(0, 16, stride=2), :] = jnp.where(left[:16], even, pltpu.roll(odd, 64, 1))
        turn[pl.ds(1, 16, stride=2), :] = jnp.where(left[:16], pltpu.roll(even, 64, 1), odd)
        turned = turn[...].T
        unit = (row + 128 * j == base + (lane - 32) * 16).astype(F32)
        right = jnp.where(lane < 32, turned, jnp.where(lane < 36, unit, 0.0))
        full[128 * j : 128 * j + 128, 512:640] = right
    product = None
    diagonal = full[0:128, 0:128]
    for k in range(4):
        s = slice(128 * k, 128 * k + 128)
        tiles = inverse_factor([diagonal[8 * t : 8 * t + 8, :] for t in range(16)])
        for t in range(16):
            inv[k, 8 * t : 8 * t + 8, :] = tiles[t]
        after = 128 * k + 128
        if k < 3:
            n = slice(after, after + 128)
            strip = dot(inv[k], full[s, n], 1, 0)
            full[s, n] = strip
            diagonal = full[n, n] - dot(strip, strip, 0, 0)
            rest = slice(after + 128, 640)
            full[s, rest] = dot(inv[k], full[s, rest], 1, 0)
            full[n, rest] -= dot(full[s, n], full[s, rest], 0, 0)
            for i in range(k + 2, 4):
                to = slice(128 * i, 128 * i + 128)
                full[to, 128 * i : 640] -= dot(full[s, to], full[s, 128 * i : 640], 0, 0)
        else:
            full[s, after:640] = dot(inv[k], full[s, after:640], 1, 0)
        part = dot(full[s, 512:640], full[s, 512:640], 0, 0)
        product = part if product is None else product + part
    out[...] = product[32:36, 0:32]


def solve(pos, mine, theirs):
    return pl.pallas_call(
        solve_kernel,
        out_shape=shape(4, 32),
        in_specs=[SM] + [VM] * 2,
        out_specs=VM,
        scratch_shapes=[
            pltpu.VMEM((512, 640), F32),
            pltpu.VMEM((4, 128, 128), F32),
            pltpu.VMEM((128, 128), F32),
        ],
        compiler_params=params(),
        name="solve",
    )(pos, mine, theirs)


def index(y, z, c):
    return (y * NZ + z) * NC + c


def exchange(value, groups):
    return lax.all_to_all(value, "dp", 0, 0, axis_index_groups=groups, tiled=True)


def swap(value, partner):
    pairs = [
        (index(*partner(y, z, c)), index(y, z, c))
        for y in range(NY)
        for z in range(NZ)
        for c in range(NC)
    ]
    return lax.ppermute(value, "dp", pairs)


def other_core(y, z, c):
    return y, z, 1 - c


def shards(tg, ta, qg, qa, of, inf, tlen, qlen):
    ys, zs, cs = range(NY), range(NZ), range(NC)
    line_groups = [[index(y, z, c) for z in zs] for y in ys for c in cs]
    y_groups = [[index(y, z, c) for y in ys] for z in zs for c in cs]
    pos = lax.axis_index("dp").astype(jnp.int32).reshape(1)
    parts = project(tg, ta, qg, qa, of, inf)
    parts = lax.all_to_all(parts, "mp", 0, 0, tiled=True)
    zcopies, own = sketch(tlen, qlen, parts)
    pair = jnp.concatenate([own, swap(own, other_core)], axis=0)
    line = exchange(zcopies, line_groups).reshape(NZ * 32, 128)
    near = jnp.concatenate([pair, swap(pair, lambda y, z, c: (y ^ 1, z, c))], axis=0)
    away = swap(near, lambda y, z, c: (NY - 1 - y, z, c))
    tiles = lax.all_to_all(tile(pos, line, near, away), "mp", 0, 0, tiled=True)
    panels = panel(exchange(add(tiles), line_groups))
    mine = exchange(panels, y_groups)
    return solve(pos, mine, swap(mine, other_core))


def solution(mesh):
    return jax.shard_map(
        shards,
        mesh=mesh,
        in_specs=(
            P("dp", None, "mp"),
            P("dp", None, "mp"),
            P("dp", None, "mp"),
            P("dp", None, "mp"),
            P(None, "mp"),
            P(None, "mp"),
            P("dp"),
            P("dp"),
        ),
        out_specs=P("dp", "mp"),
        check_vma=False,
    )
```

```python
import jax
import jax.numpy as jnp
from jax import lax
from jax.experimental import pallas as pl
from jax.experimental.pallas import tpu as pltpu
from jax.sharding import PartitionSpec as P

damping = 2.0
F32 = jnp.float32
HIGHEST = lax.Precision.HIGHEST
MB = 1024 * 1024

NY, NZ, NC = 4, 16, 2
VM = pl.BlockSpec(memory_space=pltpu.VMEM)
SM = pl.BlockSpec(memory_space=pltpu.SMEM)
ANY = pl.BlockSpec(memory_space=pl.ANY)


def params(limit=40 * MB):
    return pltpu.CompilerParams(vmem_limit_bytes=limit)


def shape(*sizes):
    return jax.ShapeDtypeStruct(sizes, F32)


def dot(a, b, ca, cb, precision=HIGHEST):
    return lax.dot_general(
        a, b, (((ca,), (cb,)), ((), ())), precision=precision, preferred_element_type=F32
    )


def lanes(*sizes):
    return lax.broadcasted_iota(jnp.int32, sizes, 1)


CHUNKS = 4


def project_kernel(tg, ta, qg, qa, of, inf, out, g, a, fo, fi, acc, sem):
    copies = []

    def start(src, dst):
        copy = pltpu.make_async_copy(src, dst, sem.at[len(copies)])
        copy.start()
        copies.append(copy)

    start(inf.at[0:32], fi.at[32:64])
    start(inf.at[32:64], fi.at[96:128])
    start(ta, a.at[0:4])
    start(qa, a.at[4:5])
    start(of.at[0:32], fo.at[0:32])
    start(of.at[32:64], fo.at[64:96])
    width = g.shape[2] // CHUNKS
    for j in range(CHUNKS):
        s = slice(j * width, (j + 1) * width)
        start(tg.at[:, :, s], g.at[0:4, :, s])
        start(qg.at[:, :, s], g.at[4:5, :, s])
    for at in (0, 64):
        fi[at : at + 32, :] = jnp.zeros((32, fi.shape[1]), fi.dtype)
        fo[at + 32 : at + 64, :] = jnp.zeros((32, fo.shape[1]), fo.dtype)
    for copy in copies[:4]:
        copy.wait()
    acc[...] = dot(a[...].reshape(320, a.shape[2]), fi[...], 1, 1, None)
    copies[4].wait()
    copies[5].wait()
    for j in range(CHUNKS):
        copies[6 + 2 * j].wait()
        copies[7 + 2 * j].wait()
        s = slice(j * width, (j + 1) * width)
        acc[...] += dot(g[:, :, s].reshape(320, width), fo[:, s], 1, 1, None)
    for low, high, to, n in ((0, 128, 0, 128), (256, 288, 128, 32)):
        left = lanes(n, 128) < 64
        first = acc[low : low + n, :]
        second = acc[high : high + n, :]
        for p in range(4):
            one = pltpu.roll(first, (128 - 32 * p) % 128, 1) if p else first
            two = pltpu.roll(second, (64 - 32 * p) % 128, 1) if p != 2 else second
            out[p, to : to + n, :] = jnp.where(left, one, two)


def project(tg, ta, qg, qa, of, inf):
    kg, ka = tg.shape[2], ta.shape[2]
    return pl.pallas_call(
        project_kernel,
        out_shape=shape(4, 160, 128),
        in_specs=[ANY] * 6,
        out_specs=VM,
        scratch_shapes=[
            pltpu.VMEM((5, 64, kg), jnp.bfloat16),
            pltpu.VMEM((5, 64, ka), jnp.bfloat16),
            pltpu.VMEM((128, kg), jnp.bfloat16),
            pltpu.VMEM((128, ka), jnp.bfloat16),
            pltpu.VMEM((320, 128), F32),
            pltpu.SemaphoreType.DMA((6 + 2 * CHUNKS,)),
        ],
        compiler_params=params(56 * MB),
        name="project",
    )(tg, ta, qg, qa, of, inf)


def sketch_kernel(tlen, qlen, parts, zcopies, own, square):
    lane = lanes(8, 128)

    def fold(row, col):
        total = None
        for g in range(4):
            piece = square[row + 8 * g : row + 8 * g + 8, :]
            shift = (32 * g - col) % 128
            piece = pltpu.roll(piece, shift, 1) if shift else piece
            piece = jnp.where((lane >= 32 * g) & (lane < 32 * g + 32), piece, 0.0)
            total = piece if total is None else total + piece
        return total

    def emit(e, tile):
        for t in range(NZ):
            if e < 4:
                zcopies[t, 8 * e : 8 * e + 8, :] = tile
        own[8 * e : 8 * e + 8, :] = tile

    def outer(low, n, weight):
        s = slice(low, low + n)
        x = (parts[0, s, :] + parts[1, s, :]) + (parts[2, s, :] + parts[3, s, :])
        square[...] = dot(x * weight, x, 0, 0)

    token = lax.broadcasted_iota(jnp.int32, (64, 128), 0)
    left = lanes(64, 128) < 64
    for e in range(2):
        length = jnp.where(left, tlen[e], tlen[e + 2])
        weight = (token < length).astype(F32) / length.astype(F32)
        outer(64 * e, 64, weight)
        emit(e, fold(0, 32))
        emit(e + 2, fold(64, 96))
    token = token[0:32] + jnp.where(left[0:32], 0, 32)
    outer(128, 32, (token < qlen[0]).astype(F32))
    emit(4, fold(0, 32) + fold(64, 96))


def sketch(tlen, qlen, parts):
    return pl.pallas_call(
        sketch_kernel,
        out_shape=(shape(NZ, 32, 128), shape(40, 128)),
        in_specs=[SM] * 2 + [VM],
        out_specs=(VM, VM),
        scratch_shapes=[pltpu.VMEM((128, 128), F32)],
        compiler_params=params(),
        name="sketch",
    )(tlen, qlen, parts)


def tile_kernel(pos, line, near, away, out, cols, held):
    y = pos[0] // (NZ * NC)
    c = lax.rem(pos[0], NC)
    for t, pairs in enumerate((near, near, away, away)):
        at = y if t < 2 else NY - 1 - y
        at = at if t % 2 == 0 else at + 1 - 2 * lax.rem(at, 2)
        for h in range(2):
            b = at * NC + lax.rem(c + h, NC)
            start = pl.multiple_of(b * 40, 8)
            row = 80 * (t % 2) + 40 * h
            cols[pl.ds(start, 40), :] = pairs[row : row + 40, :]
    total = None
    for s in range(8):
        rows = [line[pl.ds(8 * i + s, NZ, stride=32), :] for i in range(4)]
        part = dot(cols[pl.ds(s, 40, stride=8), :], jnp.concatenate(rows, axis=0), 1, 1)
        total = part if total is None else total + part
    held[:, 0:64] = total
    held[:, 64:128] = total
    for p in range(4):
        out[p, 16:24, :] = jnp.zeros((8, 128), F32)
        for h in range(2):
            s = slice(64 * h, 64 * h + 64)
            for g in range(4):
                row = 5 * (4 * h + g)
                out[p, 4 * g : 4 * g + 4, s] = held[row : row + 4, s]
            row = 5 * (2 * p + h) + 4
            out[p, 16:17, s] = held[row : row + 1, s]


def tile(pos, line, near, away):
    return pl.pallas_call(
        tile_kernel,
        out_shape=shape(4, 24, 128),
        in_specs=[SM] + [VM] * 3,
        out_specs=VM,
        scratch_shapes=[pltpu.VMEM((320, 128), F32), pltpu.VMEM((40, 128), F32)],
        compiler_params=params(),
        name="tile",
    )(pos, line, near, away)


def add_kernel(parts, out):
    total = (parts[0] + parts[1]) + (parts[2] + parts[3])
    for t in range(NZ):
        out[t] = total


def add(parts):
    return pl.pallas_call(
        add_kernel,
        out_shape=shape(NZ, 24, 128),
        in_specs=[VM],
        out_specs=VM,
        compiler_params=params(),
        name="add",
    )(parts)


def panel_kernel(parts, out):
    for z in range(NZ):
        both = parts[z, 0:16, :]
        query = parts[z, 16:17, :]
        for t in range(NY):
            out[t, pl.ds(z, 16, stride=NZ), :] = both
            out[t, 256 + z : 257 + z, :] = query


def panel(parts):
    return pl.pallas_call(
        panel_kernel,
        out_shape=shape(NY, 272, 128),
        in_specs=[VM],
        out_specs=VM,
        compiler_params=params(),
        name="panel",
    )(parts)


def rank16(a, b):
    def parts(x):
        one = x.astype(jnp.bfloat16)
        x = x - one.astype(F32)
        two = x.astype(jnp.bfloat16)
        return one, two, (x - two.astype(F32)).astype(jnp.bfloat16)

    a1, a2, a3 = parts(a)
    b1, b2, b3 = parts(b)
    left = jnp.concatenate([a1, a1, a2, a2, a1, a3], axis=0)
    right = jnp.concatenate([b1, b2, b1, b2, b3, b1], axis=0)
    return dot(left, right, 0, 0, None)


def inverse_factor(tiles):
    lane = lanes(8, 128)
    sub = lax.broadcasted_iota(jnp.int32, (8, 128), 0)
    count = len(tiles)
    tiles = list(tiles)

    def inside(q):
        return (lane >= 8 * q) & (lane < 8 * q + 8)

    def column(r, q, c):
        return jnp.broadcast_to(tiles[r][:, 8 * q + c : 8 * q + c + 1], (8, 128))

    def stack(rows):
        merged = rows[0]
        for p in range(1, 8):
            merged = jnp.where(sub == p, rows[p], merged)
        return merged

    def panel_of(q):
        block = tiles[q]
        a = {}
        for c in range(8):
            whole = column(q, q, c)
            for p in range(c, 8):
                a[p, c] = jnp.broadcast_to(whole[p : p + 1, :], (8, 128))
        mult = {}
        lines, scaled, rows = [], [], []
        for p in range(0, 8, 2):
            d, o, e = a[p, p], a[p + 1, p], a[p + 1, p + 1]
            root = lax.rsqrt(d * e - o * o)
            inverse = root * root
            for k in range(p + 2, 8):
                mult[k, p] = (a[k, p] * e - a[k, p + 1] * o) * inverse
                mult[k, p + 1] = (a[k, p + 1] * d - a[k, p] * o) * inverse
            for k in range(p + 2, 8):
                for c in range(p + 2, k + 1):
                    a[k, c] = a[k, c] - (mult[k, p] * a[c, p] + mult[k, p + 1] * a[c, p + 1])
            for r in (p, p + 1):
                unit = (lane == 8 * q + r).astype(F32)
                line = jnp.broadcast_to(block[r : r + 1, :], (8, 128))
                line = jnp.where(inside(q), unit, line)
                for k in range(p):
                    line = line - mult[r, k] * lines[k]
                lines.append(line)
            low, high = lines[p], lines[p + 1]
            turned = high * d - low * o
            scaled.append((low * e - high * o) * inverse)
            scaled.append(turned * inverse)
            top = lax.rsqrt(d)
            rows.append(low * top)
            rows.append(turned * (top * root))
        tiles[q] = stack(rows)
        return block, mult, scaled

    def update_next(q, mult, scaled):
        rest = jnp.where(inside(q), 0.0, tiles[q + 1])
        cols = []
        for p in range(0, 8, 2):
            for r in (p, p + 1):
                col = column(q + 1, q, r)
                for k in range(p):
                    col = col - mult[r, k] * cols[k]
                cols.append(col)
            rest = rest - (cols[p] * scaled[p] + cols[p + 1] * scaled[p + 1])
        tiles[q + 1] = rest

    def substitute(mult, scaled):
        back = list(scaled)
        for p in range(5, -1, -1):
            for k in range(7, p + 1 - p % 2, -1):
                back[p] = back[p] - mult[k, p] * back[k]
        return back

    for q in range(0, count, 2):
        block0, mult0, scaled0 = panel_of(q)
        update_next(q, mult0, scaled0)
        if q + 2 < count:
            back0 = substitute(mult0, scaled0)
            other = jnp.where(inside(q), 0.0, tiles[q + 2])
            for c in range(8):
                other = other - column(q + 2, q, c) * back0[c]
            tiles[q + 2] = other
        block1, mult1, scaled1 = panel_of(q + 1)
        if q + 2 < count:
            update_next(q + 1, mult1, scaled1)
            back1 = substitute(mult1, scaled1)
            both = inside(q) | inside(q + 1)
            right = jnp.concatenate(
                [jnp.where(inside(q + 1), 0.0, stack(back0)), stack(back1)], axis=0
            )
            far = rank16(jnp.concatenate([block0, block1], axis=0), right)
            for r in range(q + 3, count):
                tiles[r] = jnp.where(both, 0.0, tiles[r]) - far[8 * r : 8 * r + 8, :]
    for q in range(count):
        tiles[q] = jnp.where(lane <= sub + 8 * q, tiles[q], 0.0)
    return tiles


def solve_kernel(pos, mine, theirs, out, full, inv, turn):
    d = pos[0]
    y = d // (NZ * NC)
    z = lax.rem(d // NC, NZ)
    c = lax.rem(d, NC)
    base = (y * NC + c) * 64 + z
    first = c == 0
    lane = lanes(128, 128)
    row = lax.broadcasted_iota(jnp.int32, (128, 128), 0)
    left = lane < 64
    eye = (lane == row).astype(F32) * damping

    for j in range(NY):
        for k in range(j + 1):
            s = slice(128 * (k % 2), 128 * (k % 2) + 128)
            even = jnp.where(first, mine[j, s, :], theirs[j, s, :])
            odd = jnp.where(first, theirs[j, s, :], mine[j, s, :])
            if k < 2:
                block = jnp.where(left, even, pltpu.roll(odd, 64, 1))
            else:
                block = jnp.where(left, pltpu.roll(even, 64, 1), odd)
            if j == k:
                block = block + eye
            full[128 * k : 128 * k + 128, 128 * j : 128 * j + 128] = block
        for k in range(j + 1, NY):
            full[128 * k : 128 * k + 128, 128 * j : 128 * j + 128] = jnp.zeros((128, 128), F32)
        even = jnp.where(first, mine[j, 256:272, :], theirs[j, 256:272, :])
        odd = jnp.where(first, theirs[j, 256:272, :], mine[j, 256:272, :])
        turn[pl.ds(0, 16, stride=2), :] = jnp.where(left[:16], even, pltpu.roll(odd, 64, 1))
        turn[pl.ds(1, 16, stride=2), :] = jnp.where(left[:16], pltpu.roll(even, 64, 1), odd)
        turned = turn[...].T
        unit = (row + 128 * j == base + (lane - 32) * 16).astype(F32)
        right = jnp.where(lane < 32, turned, jnp.where(lane < 36, unit, 0.0))
        full[128 * j : 128 * j + 128, 512:640] = right
    def step(k, carry):
        at = pl.multiple_of(k * 128, 128)
        s = pl.ds(at, 128)
        tiles = inverse_factor([full[pl.ds(at + 8 * t, 8), s] for t in range(16)])
        for t in range(16):
            inv[8 * t : 8 * t + 8, :] = tiles[t]
        full[s, :] = dot(inv[...], full[s, :], 1, 0)

        def trail(i, inner):
            to = pl.ds(pl.multiple_of(i * 128, 128), 128)
            full[to, :] -= dot(full[s, to], full[s, :], 0, 0)
            return inner

        return lax.fori_loop(k + 1, 4, trail, carry)

    lax.fori_loop(0, 4, step, 0)
    product = dot(full[:, 512:640], full[:, 512:640], 0, 0)
    out[...] = product[32:36, 0:32]


def solve(pos, mine, theirs):
    return pl.pallas_call(
        solve_kernel,
        out_shape=shape(4, 32),
        in_specs=[SM] + [VM] * 2,
        out_specs=VM,
        scratch_shapes=[
            pltpu.VMEM((512, 640), F32),
            pltpu.VMEM((128, 128), F32),
            pltpu.VMEM((128, 128), F32),
        ],
        compiler_params=params(),
        name="solve",
    )(pos, mine, theirs)


def index(y, z, c):
    return (y * NZ + z) * NC + c


def exchange(value, groups):
    return lax.all_to_all(value, "dp", 0, 0, axis_index_groups=groups, tiled=True)


def swap(value, partner):
    pairs = [
        (index(*partner(y, z, c)), index(y, z, c))
        for y in range(NY)
        for z in range(NZ)
        for c in range(NC)
    ]
    return lax.ppermute(value, "dp", pairs)


def other_core(y, z, c):
    return y, z, 1 - c


def shards(tg, ta, qg, qa, of, inf, tlen, qlen):
    ys, zs, cs = range(NY), range(NZ), range(NC)
    line_groups = [[index(y, z, c) for z in zs] for y in ys for c in cs]
    y_groups = [[index(y, z, c) for y in ys] for z in zs for c in cs]
    pos = lax.axis_index("dp").astype(jnp.int32).reshape(1)
    parts = project(tg, ta, qg, qa, of, inf)
    parts = lax.all_to_all(parts, "mp", 0, 0, tiled=True)
    zcopies, own = sketch(tlen, qlen, parts)
    pair = jnp.concatenate([own, swap(own, other_core)], axis=0)
    line = exchange(zcopies, line_groups).reshape(NZ * 32, 128)
    near = jnp.concatenate([pair, swap(pair, lambda y, z, c: (y ^ 1, z, c))], axis=0)
    away = swap(near, lambda y, z, c: (NY - 1 - y, z, c))
    tiles = lax.all_to_all(tile(pos, line, near, away), "mp", 0, 0, tiled=True)
    panels = panel(exchange(add(tiles), line_groups))
    mine = exchange(panels, y_groups)
    return solve(pos, mine, swap(mine, other_core))


def solution(mesh):
    return jax.shard_map(
        shards,
        mesh=mesh,
        in_specs=(
            P("dp", None, "mp"),
            P("dp", None, "mp"),
            P("dp", None, "mp"),
            P("dp", None, "mp"),
            P(None, "mp"),
            P(None, "mp"),
            P("dp"),
            P("dp"),
        ),
        out_specs=P("dp", "mp"),
        check_vma=False,
    )
```

```python
import jax
import jax.numpy as jnp
from jax import lax
from jax.experimental import pallas as pl
from jax.experimental.pallas import tpu as pltpu
from jax.sharding import PartitionSpec as P

damping = 2.0
F32 = jnp.float32
HIGHEST = lax.Precision.HIGHEST
MB = 1024 * 1024

NY, NZ, NC = 4, 16, 2
VM = pl.BlockSpec(memory_space=pltpu.VMEM)
SM = pl.BlockSpec(memory_space=pltpu.SMEM)
ANY = pl.BlockSpec(memory_space=pl.ANY)


def params(limit=40 * MB):
    return pltpu.CompilerParams(vmem_limit_bytes=limit)


def shape(*sizes):
    return jax.ShapeDtypeStruct(sizes, F32)


def dot(a, b, ca, cb, precision=HIGHEST):
    return lax.dot_general(
        a, b, (((ca,), (cb,)), ((), ())), precision=precision, preferred_element_type=F32
    )


def lanes(*sizes):
    return lax.broadcasted_iota(jnp.int32, sizes, 1)


CHUNKS = 4


def project_kernel(tg, ta, qg, qa, of, inf, out, g, a, fo, fi, acc, sem):
    copies = []

    def start(src, dst):
        copy = pltpu.make_async_copy(src, dst, sem.at[len(copies)])
        copy.start()
        copies.append(copy)

    start(inf.at[0:32], fi.at[32:64])
    start(inf.at[32:64], fi.at[96:128])
    start(ta, a.at[0:4])
    start(qa, a.at[4:5])
    start(of.at[0:32], fo.at[0:32])
    start(of.at[32:64], fo.at[64:96])
    width = g.shape[2] // CHUNKS
    for j in range(CHUNKS):
        s = slice(j * width, (j + 1) * width)
        start(tg.at[:, :, s], g.at[0:4, :, s])
        start(qg.at[:, :, s], g.at[4:5, :, s])
    for at in (0, 64):
        fi[at : at + 32, :] = jnp.zeros((32, fi.shape[1]), fi.dtype)
        fo[at + 32 : at + 64, :] = jnp.zeros((32, fo.shape[1]), fo.dtype)
    for copy in copies[:4]:
        copy.wait()
    acc[...] = dot(a[...].reshape(320, a.shape[2]), fi[...], 1, 1, None)
    copies[4].wait()
    copies[5].wait()
    for j in range(CHUNKS):
        copies[6 + 2 * j].wait()
        copies[7 + 2 * j].wait()
        s = slice(j * width, (j + 1) * width)
        acc[...] += dot(g[:, :, s].reshape(320, width), fo[:, s], 1, 1, None)
    for low, high, to, n in ((0, 128, 0, 128), (256, 288, 128, 32)):
        left = lanes(n, 128) < 64
        first = acc[low : low + n, :]
        second = acc[high : high + n, :]
        for p in range(4):
            one = pltpu.roll(first, (128 - 32 * p) % 128, 1) if p else first
            two = pltpu.roll(second, (64 - 32 * p) % 128, 1) if p != 2 else second
            out[p, to : to + n, :] = jnp.where(left, one, two)


def project(tg, ta, qg, qa, of, inf):
    kg, ka = tg.shape[2], ta.shape[2]
    return pl.pallas_call(
        project_kernel,
        out_shape=shape(4, 160, 128),
        in_specs=[ANY] * 6,
        out_specs=VM,
        scratch_shapes=[
            pltpu.VMEM((5, 64, kg), jnp.bfloat16),
            pltpu.VMEM((5, 64, ka), jnp.bfloat16),
            pltpu.VMEM((128, kg), jnp.bfloat16),
            pltpu.VMEM((128, ka), jnp.bfloat16),
            pltpu.VMEM((320, 128), F32),
            pltpu.SemaphoreType.DMA((6 + 2 * CHUNKS,)),
        ],
        compiler_params=params(56 * MB),
        name="project",
    )(tg, ta, qg, qa, of, inf)


def sketch_kernel(tlen, qlen, parts, zcopies, own, square):
    lane = lanes(8, 128)

    def fold(row, col):
        total = None
        for g in range(4):
            piece = square[row + 8 * g : row + 8 * g + 8, :]
            shift = (32 * g - col) % 128
            piece = pltpu.roll(piece, shift, 1) if shift else piece
            piece = jnp.where((lane >= 32 * g) & (lane < 32 * g + 32), piece, 0.0)
            total = piece if total is None else total + piece
        return total

    def emit(e, tile):
        for t in range(NZ):
            if e < 4:
                zcopies[t, 8 * e : 8 * e + 8, :] = tile
        own[8 * e : 8 * e + 8, :] = tile

    def outer(low, n, weight):
        s = slice(low, low + n)
        x = (parts[0, s, :] + parts[1, s, :]) + (parts[2, s, :] + parts[3, s, :])
        square[...] = dot(x * weight, x, 0, 0)

    token = lax.broadcasted_iota(jnp.int32, (64, 128), 0)
    left = lanes(64, 128) < 64
    for e in range(2):
        length = jnp.where(left, tlen[e], tlen[e + 2])
        weight = (token < length).astype(F32) / length.astype(F32)
        outer(64 * e, 64, weight)
        emit(e, fold(0, 32))
        emit(e + 2, fold(64, 96))
    token = token[0:32] + jnp.where(left[0:32], 0, 32)
    outer(128, 32, (token < qlen[0]).astype(F32))
    emit(4, fold(0, 32) + fold(64, 96))


def sketch(tlen, qlen, parts):
    return pl.pallas_call(
        sketch_kernel,
        out_shape=(shape(NZ, 32, 128), shape(40, 128)),
        in_specs=[SM] * 2 + [VM],
        out_specs=(VM, VM),
        scratch_shapes=[pltpu.VMEM((128, 128), F32)],
        compiler_params=params(),
        name="sketch",
    )(tlen, qlen, parts)


def tile_kernel(pos, line, near, away, out, cols, held):
    y = pos[0] // (NZ * NC)
    c = lax.rem(pos[0], NC)
    for t, pairs in enumerate((near, near, away, away)):
        at = y if t < 2 else NY - 1 - y
        at = at if t % 2 == 0 else at + 1 - 2 * lax.rem(at, 2)
        for h in range(2):
            b = at * NC + lax.rem(c + h, NC)
            start = pl.multiple_of(b * 40, 8)
            row = 80 * (t % 2) + 40 * h
            cols[pl.ds(start, 40), :] = pairs[row : row + 40, :]
    total = None
    for s in range(8):
        rows = [line[pl.ds(8 * i + s, NZ, stride=32), :] for i in range(4)]
        part = dot(cols[pl.ds(s, 40, stride=8), :], jnp.concatenate(rows, axis=0), 1, 1)
        total = part if total is None else total + part
    held[:, 0:64] = total
    held[:, 64:128] = total
    for p in range(4):
        out[p, 16:24, :] = jnp.zeros((8, 128), F32)
        for h in range(2):
            s = slice(64 * h, 64 * h + 64)
            for g in range(4):
                row = 5 * (4 * h + g)
                out[p, 4 * g : 4 * g + 4, s] = held[row : row + 4, s]
            row = 5 * (2 * p + h) + 4
            out[p, 16:17, s] = held[row : row + 1, s]


def tile(pos, line, near, away):
    return pl.pallas_call(
        tile_kernel,
        out_shape=shape(4, 24, 128),
        in_specs=[SM] + [VM] * 3,
        out_specs=VM,
        scratch_shapes=[pltpu.VMEM((320, 128), F32), pltpu.VMEM((40, 128), F32)],
        compiler_params=params(),
        name="tile",
    )(pos, line, near, away)


def add_kernel(parts, out):
    total = (parts[0] + parts[1]) + (parts[2] + parts[3])
    for t in range(NZ):
        out[t] = total


def add(parts):
    return pl.pallas_call(
        add_kernel,
        out_shape=shape(NZ, 24, 128),
        in_specs=[VM],
        out_specs=VM,
        compiler_params=params(),
        name="add",
    )(parts)


def panel_kernel(parts, out):
    for z in range(NZ):
        both = parts[z, 0:16, :]
        query = parts[z, 16:17, :]
        for t in range(NY):
            out[t, pl.ds(z, 16, stride=NZ), :] = both
            out[t, 256 + z : 257 + z, :] = query


def panel(parts):
    return pl.pallas_call(
        panel_kernel,
        out_shape=shape(NY, 272, 128),
        in_specs=[VM],
        out_specs=VM,
        compiler_params=params(),
        name="panel",
    )(parts)


def thirds(x):
    one = x.astype(jnp.bfloat16)
    x = x - one.astype(F32)
    two = x.astype(jnp.bfloat16)
    return one, two, (x - two.astype(F32)).astype(jnp.bfloat16)


def stacked(a, b, ca, cb):
    a1, a2, a3 = thirds(a)
    b1, b2, b3 = thirds(b)
    left = jnp.concatenate([a1, a1, a2, a2, a1, a3], axis=ca)
    right = jnp.concatenate([b1, b2, b1, b2, b3, b1], axis=cb)
    return dot(left, right, ca, cb, None)


def inverse_factor(tiles):
    lane = lanes(8, 128)
    sub = lax.broadcasted_iota(jnp.int32, (8, 128), 0)
    count = len(tiles)
    tiles = list(tiles)

    def inside(q):
        return (lane >= 8 * q) & (lane < 8 * q + 8)

    def column(r, q, c):
        return jnp.broadcast_to(tiles[r][:, 8 * q + c : 8 * q + c + 1], (8, 128))

    def stack(rows):
        merged = rows[0]
        for p in range(1, 8):
            merged = jnp.where(sub == p, rows[p], merged)
        return merged

    def panel_of(q):
        block = tiles[q]
        a = {}
        for c in range(8):
            whole = column(q, q, c)
            for p in range(c, 8):
                a[p, c] = jnp.broadcast_to(whole[p : p + 1, :], (8, 128))
        mult = {}
        lines, scaled, rows = [], [], []
        for p in range(0, 8, 2):
            d, o, e = a[p, p], a[p + 1, p], a[p + 1, p + 1]
            root = lax.rsqrt(d * e - o * o)
            inverse = root * root
            for k in range(p + 2, 8):
                mult[k, p] = (a[k, p] * e - a[k, p + 1] * o) * inverse
                mult[k, p + 1] = (a[k, p + 1] * d - a[k, p] * o) * inverse
            for k in range(p + 2, 8):
                for c in range(p + 2, k + 1):
                    a[k, c] = a[k, c] - (mult[k, p] * a[c, p] + mult[k, p + 1] * a[c, p + 1])
            for r in (p, p + 1):
                unit = (lane == 8 * q + r).astype(F32)
                line = jnp.broadcast_to(block[r : r + 1, :], (8, 128))
                line = jnp.where(inside(q), unit, line)
                for k in range(p):
                    line = line - mult[r, k] * lines[k]
                lines.append(line)
            low, high = lines[p], lines[p + 1]
            turned = high * d - low * o
            scaled.append((low * e - high * o) * inverse)
            scaled.append(turned * inverse)
            top = lax.rsqrt(d)
            rows.append(low * top)
            rows.append(turned * (top * root))
        tiles[q] = stack(rows)
        return block, mult, scaled

    def update_next(q, mult, scaled):
        rest = jnp.where(inside(q), 0.0, tiles[q + 1])
        cols = []
        for p in range(0, 8, 2):
            for r in (p, p + 1):
                col = column(q + 1, q, r)
                for k in range(p):
                    col = col - mult[r, k] * cols[k]
                cols.append(col)
            rest = rest - (cols[p] * scaled[p] + cols[p + 1] * scaled[p + 1])
        tiles[q + 1] = rest

    def substitute(mult, scaled):
        back = list(scaled)
        for p in range(5, -1, -1):
            for k in range(7, p + 1 - p % 2, -1):
                back[p] = back[p] - mult[k, p] * back[k]
        return back

    for q in range(0, count, 2):
        block0, mult0, scaled0 = panel_of(q)
        update_next(q, mult0, scaled0)
        if q + 2 < count:
            back0 = substitute(mult0, scaled0)
            other = jnp.where(inside(q), 0.0, tiles[q + 2])
            for c in range(8):
                other = other - column(q + 2, q, c) * back0[c]
            tiles[q + 2] = other
        block1, mult1, scaled1 = panel_of(q + 1)
        if q + 2 < count:
            update_next(q + 1, mult1, scaled1)
            back1 = substitute(mult1, scaled1)
            both = inside(q) | inside(q + 1)
            right = jnp.concatenate(
                [jnp.where(inside(q + 1), 0.0, stack(back0)), stack(back1)], axis=0
            )
            far = stacked(jnp.concatenate([block0, block1], axis=0), right, 0, 0)
            for r in range(q + 3, count):
                tiles[r] = jnp.where(both, 0.0, tiles[r]) - far[8 * r : 8 * r + 8, :]
    for q in range(count):
        tiles[q] = jnp.where(lane <= sub + 8 * q, tiles[q], 0.0)
    return tiles


def solve_kernel(pos, mine, theirs, out, full, inv, turn):
    d = pos[0]
    y = d // (NZ * NC)
    z = lax.rem(d // NC, NZ)
    c = lax.rem(d, NC)
    base = (y * NC + c) * 64 + z
    first = c == 0
    lane = lanes(128, 128)
    row = lax.broadcasted_iota(jnp.int32, (128, 128), 0)
    left = lane < 64
    eye = (lane == row).astype(F32) * damping

    for j in range(NY):
        for k in range(j + 1):
            s = slice(128 * (k % 2), 128 * (k % 2) + 128)
            even = jnp.where(first, mine[j, s, :], theirs[j, s, :])
            odd = jnp.where(first, theirs[j, s, :], mine[j, s, :])
            if k < 2:
                block = jnp.where(left, even, pltpu.roll(odd, 64, 1))
            else:
                block = jnp.where(left, pltpu.roll(even, 64, 1), odd)
            if j == k:
                block = block + eye
            full[128 * k : 128 * k + 128, 128 * j : 128 * j + 128] = block
        for k in range(j + 1, NY):
            full[128 * k : 128 * k + 128, 128 * j : 128 * j + 128] = jnp.zeros((128, 128), F32)
        even = jnp.where(first, mine[j, 256:272, :], theirs[j, 256:272, :])
        odd = jnp.where(first, theirs[j, 256:272, :], mine[j, 256:272, :])
        turn[pl.ds(0, 16, stride=2), :] = jnp.where(left[:16], even, pltpu.roll(odd, 64, 1))
        turn[pl.ds(1, 16, stride=2), :] = jnp.where(left[:16], pltpu.roll(even, 64, 1), odd)
        turned = turn[...].T
        unit = (row + 128 * j == base + (lane - 32) * 16).astype(F32)
        right = jnp.where(lane < 32, turned, jnp.where(lane < 36, unit, 0.0))
        full[128 * j : 128 * j + 128, 512:640] = right
    def step(k, carry):
        at = pl.multiple_of(k * 128, 128)
        s = pl.ds(at, 128)
        tiles = inverse_factor([full[pl.ds(at + 8 * t, 8), s] for t in range(16)])
        for t in range(16):
            inv[8 * t : 8 * t + 8, :] = tiles[t]

        for j in range(4):

            @pl.when(k == j)
            def _():
                s = slice(128 * j, 128 * j + 128)
                after = 128 * j + 128
                strip = stacked(inv[...], full[s, after:640], 1, 0)
                full[s, 512:640] = strip[:, 512 - after :]
                if j < 3:
                    turned = strip[:, : 512 - after].T
                    full[after:512, after:640] -= stacked(turned, strip, 1, 0)

        return carry

    lax.fori_loop(0, 4, step, 0)
    right = full[:, 512:640]
    out[...] = stacked(right.T[32:40, :], right, 1, 0)[0:4, 0:32]


def solve(pos, mine, theirs):
    return pl.pallas_call(
        solve_kernel,
        out_shape=shape(4, 32),
        in_specs=[SM] + [VM] * 2,
        out_specs=VM,
        scratch_shapes=[
            pltpu.VMEM((512, 640), F32),
            pltpu.VMEM((128, 128), F32),
            pltpu.VMEM((128, 128), F32),
        ],
        compiler_params=params(),
        name="solve",
    )(pos, mine, theirs)


def index(y, z, c):
    return (y * NZ + z) * NC + c


def exchange(value, groups):
    return lax.all_to_all(value, "dp", 0, 0, axis_index_groups=groups, tiled=True)


def swap(value, partner):
    pairs = [
        (index(*partner(y, z, c)), index(y, z, c))
        for y in range(NY)
        for z in range(NZ)
        for c in range(NC)
    ]
    return lax.ppermute(value, "dp", pairs)


def other_core(y, z, c):
    return y, z, 1 - c


def shards(tg, ta, qg, qa, of, inf, tlen, qlen):
    ys, zs, cs = range(NY), range(NZ), range(NC)
    line_groups = [[index(y, z, c) for z in zs] for y in ys for c in cs]
    y_groups = [[index(y, z, c) for y in ys] for z in zs for c in cs]
    pos = lax.axis_index("dp").astype(jnp.int32).reshape(1)
    parts = project(tg, ta, qg, qa, of, inf)
    parts = lax.all_to_all(parts, "mp", 0, 0, tiled=True)
    zcopies, own = sketch(tlen, qlen, parts)
    pair = jnp.concatenate([own, swap(own, other_core)], axis=0)
    line = exchange(zcopies, line_groups).reshape(NZ * 32, 128)
    near = jnp.concatenate([pair, swap(pair, lambda y, z, c: (y ^ 1, z, c))], axis=0)
    away = swap(near, lambda y, z, c: (NY - 1 - y, z, c))
    tiles = lax.all_to_all(tile(pos, line, near, away), "mp", 0, 0, tiled=True)
    panels = panel(exchange(add(tiles), line_groups))
    mine = exchange(panels, y_groups)
    return solve(pos, mine, swap(mine, other_core))


def solution(mesh):
    return jax.shard_map(
        shards,
        mesh=mesh,
        in_specs=(
            P("dp", None, "mp"),
            P("dp", None, "mp"),
            P("dp", None, "mp"),
            P("dp", None, "mp"),
            P(None, "mp"),
            P(None, "mp"),
            P("dp"),
            P("dp"),
        ),
        out_specs=P("dp", "mp"),
        check_vma=False,
    )
```

```python
import jax
import jax.numpy as jnp
from jax import lax
from jax.experimental import pallas as pl
from jax.experimental.pallas import tpu as pltpu
from jax.sharding import PartitionSpec as P

damping = 2.0
F32 = jnp.float32
HIGHEST = lax.Precision.HIGHEST
MB = 1024 * 1024

NY, NZ, NC = 4, 16, 2
VM = pl.BlockSpec(memory_space=pltpu.VMEM)
SM = pl.BlockSpec(memory_space=pltpu.SMEM)
ANY = pl.BlockSpec(memory_space=pl.ANY)


def params(limit=40 * MB):
    return pltpu.CompilerParams(vmem_limit_bytes=limit)


def shape(*sizes):
    return jax.ShapeDtypeStruct(sizes, F32)


def dot(a, b, ca, cb, precision=HIGHEST):
    return lax.dot_general(
        a, b, (((ca,), (cb,)), ((), ())), precision=precision, preferred_element_type=F32
    )


def lanes(*sizes):
    return lax.broadcasted_iota(jnp.int32, sizes, 1)


CHUNKS = 4


def project_kernel(tg, ta, qg, qa, of, inf, out, g, a, fo, fi, acc, sem):
    copies = []

    def start(src, dst):
        copy = pltpu.make_async_copy(src, dst, sem.at[len(copies)])
        copy.start()
        copies.append(copy)

    start(inf.at[0:32], fi.at[32:64])
    start(inf.at[32:64], fi.at[96:128])
    start(ta, a.at[0:4])
    start(qa, a.at[4:5])
    start(of.at[0:32], fo.at[0:32])
    start(of.at[32:64], fo.at[64:96])
    width = g.shape[2] // CHUNKS
    for j in range(CHUNKS):
        s = slice(j * width, (j + 1) * width)
        start(tg.at[:, :, s], g.at[0:4, :, s])
        start(qg.at[:, :, s], g.at[4:5, :, s])
    for at in (0, 64):
        fi[at : at + 32, :] = jnp.zeros((32, fi.shape[1]), fi.dtype)
        fo[at + 32 : at + 64, :] = jnp.zeros((32, fo.shape[1]), fo.dtype)
    for copy in copies[:4]:
        copy.wait()
    acc[...] = dot(a[...].reshape(320, a.shape[2]), fi[...], 1, 1, None)
    copies[4].wait()
    copies[5].wait()
    for j in range(CHUNKS):
        copies[6 + 2 * j].wait()
        copies[7 + 2 * j].wait()
        s = slice(j * width, (j + 1) * width)
        acc[...] += dot(g[:, :, s].reshape(320, width), fo[:, s], 1, 1, None)
    for low, high, to, n in ((0, 128, 0, 128), (256, 288, 128, 32)):
        left = lanes(n, 128) < 64
        first = acc[low : low + n, :]
        second = acc[high : high + n, :]
        for p in range(4):
            one = pltpu.roll(first, (128 - 32 * p) % 128, 1) if p else first
            two = pltpu.roll(second, (64 - 32 * p) % 128, 1) if p != 2 else second
            out[p, to : to + n, :] = jnp.where(left, one, two)


def project(tg, ta, qg, qa, of, inf):
    kg, ka = tg.shape[2], ta.shape[2]
    return pl.pallas_call(
        project_kernel,
        out_shape=shape(4, 160, 128),
        in_specs=[ANY] * 6,
        out_specs=VM,
        scratch_shapes=[
            pltpu.VMEM((5, 64, kg), jnp.bfloat16),
            pltpu.VMEM((5, 64, ka), jnp.bfloat16),
            pltpu.VMEM((128, kg), jnp.bfloat16),
            pltpu.VMEM((128, ka), jnp.bfloat16),
            pltpu.VMEM((320, 128), F32),
            pltpu.SemaphoreType.DMA((6 + 2 * CHUNKS,)),
        ],
        compiler_params=params(56 * MB),
        name="project",
    )(tg, ta, qg, qa, of, inf)


def sketch_kernel(tlen, qlen, parts, zcopies, own, square):
    lane = lanes(8, 128)

    def fold(row, col):
        total = None
        for g in range(4):
            piece = square[row + 8 * g : row + 8 * g + 8, :]
            shift = (32 * g - col) % 128
            piece = pltpu.roll(piece, shift, 1) if shift else piece
            piece = jnp.where((lane >= 32 * g) & (lane < 32 * g + 32), piece, 0.0)
            total = piece if total is None else total + piece
        return total

    def emit(e, tile):
        for t in range(NZ):
            if e < 4:
                zcopies[t, 8 * e : 8 * e + 8, :] = tile
        own[8 * e : 8 * e + 8, :] = tile

    def outer(low, n, weight):
        s = slice(low, low + n)
        x = (parts[0, s, :] + parts[1, s, :]) + (parts[2, s, :] + parts[3, s, :])
        square[...] = dot(x * weight, x, 0, 0)

    token = lax.broadcasted_iota(jnp.int32, (64, 128), 0)
    left = lanes(64, 128) < 64
    for e in range(2):
        length = jnp.where(left, tlen[e], tlen[e + 2])
        weight = (token < length).astype(F32) / length.astype(F32)
        outer(64 * e, 64, weight)
        emit(e, fold(0, 32))
        emit(e + 2, fold(64, 96))
    token = token[0:32] + jnp.where(left[0:32], 0, 32)
    outer(128, 32, (token < qlen[0]).astype(F32))
    emit(4, fold(0, 32) + fold(64, 96))


def sketch(tlen, qlen, parts):
    return pl.pallas_call(
        sketch_kernel,
        out_shape=(shape(NZ, 32, 128), shape(40, 128)),
        in_specs=[SM] * 2 + [VM],
        out_specs=(VM, VM),
        scratch_shapes=[pltpu.VMEM((128, 128), F32)],
        compiler_params=params(),
        name="sketch",
    )(tlen, qlen, parts)


def tile_kernel(pos, line, near, away, out, cols, held):
    y = pos[0] // (NZ * NC)
    c = lax.rem(pos[0], NC)
    for t, pairs in enumerate((near, near, away, away)):
        at = y if t < 2 else NY - 1 - y
        at = at if t % 2 == 0 else at + 1 - 2 * lax.rem(at, 2)
        for h in range(2):
            b = at * NC + lax.rem(c + h, NC)
            start = pl.multiple_of(b * 40, 8)
            row = 80 * (t % 2) + 40 * h
            cols[pl.ds(start, 40), :] = pairs[row : row + 40, :]
    total = None
    for s in range(8):
        rows = [line[pl.ds(8 * i + s, NZ, stride=32), :] for i in range(4)]
        part = dot(cols[pl.ds(s, 40, stride=8), :], jnp.concatenate(rows, axis=0), 1, 1)
        total = part if total is None else total + part
    held[:, 0:64] = total
    held[:, 64:128] = total
    for p in range(4):
        out[p, 16:24, :] = jnp.zeros((8, 128), F32)
        for h in range(2):
            s = slice(64 * h, 64 * h + 64)
            for g in range(4):
                row = 5 * (4 * h + g)
                out[p, 4 * g : 4 * g + 4, s] = held[row : row + 4, s]
            row = 5 * (2 * p + h) + 4
            out[p, 16:17, s] = held[row : row + 1, s]


def tile(pos, line, near, away):
    return pl.pallas_call(
        tile_kernel,
        out_shape=shape(4, 24, 128),
        in_specs=[SM] + [VM] * 3,
        out_specs=VM,
        scratch_shapes=[pltpu.VMEM((320, 128), F32), pltpu.VMEM((40, 128), F32)],
        compiler_params=params(),
        name="tile",
    )(pos, line, near, away)


def add_kernel(parts, out):
    total = (parts[0] + parts[1]) + (parts[2] + parts[3])
    for t in range(NZ):
        out[t] = total


def add(parts):
    return pl.pallas_call(
        add_kernel,
        out_shape=shape(NZ, 24, 128),
        in_specs=[VM],
        out_specs=VM,
        compiler_params=params(),
        name="add",
    )(parts)


def panel_kernel(parts, out):
    for z in range(NZ):
        both = parts[z, 0:16, :]
        query = parts[z, 16:17, :]
        for t in range(NY):
            out[t, pl.ds(z, 16, stride=NZ), :] = both
            out[t, 256 + z : 257 + z, :] = query


def panel(parts):
    return pl.pallas_call(
        panel_kernel,
        out_shape=shape(NY, 272, 128),
        in_specs=[VM],
        out_specs=VM,
        compiler_params=params(),
        name="panel",
    )(parts)


def thirds(x):
    one = x.astype(jnp.bfloat16)
    x = x - one.astype(F32)
    two = x.astype(jnp.bfloat16)
    return one, two, (x - two.astype(F32)).astype(jnp.bfloat16)


def stacked(a, b, ca, cb):
    a1, a2, a3 = thirds(a)
    b1, b2, b3 = thirds(b)
    left = jnp.concatenate([a1, a1, a2, a2, a1, a3], axis=ca)
    right = jnp.concatenate([b1, b2, b1, b2, b3, b1], axis=cb)
    return dot(left, right, ca, cb, None)


def inverse_factor(tiles, hold):
    lane = lanes(8, 128)
    sub = lax.broadcasted_iota(jnp.int32, (8, 128), 0)
    count = len(tiles)
    tiles = list(tiles)

    def inside(q):
        return (lane >= 8 * q) & (lane < 8 * q + 8)

    def column(r, q, c):
        return jnp.broadcast_to(tiles[r][:, 8 * q + c : 8 * q + c + 1], (8, 128))

    def stack(rows):
        merged = rows[0]
        for p in range(1, 8):
            merged = jnp.where(sub == p, rows[p], merged)
        return merged

    def panel_of(q):
        block = tiles[q]
        hold[q, 8] = block
        a = {}
        for c in range(8):
            hold[q, c] = column(q, q, c)
            for p in range(c, 8):
                a[p, c] = jnp.broadcast_to(hold[q, c, p : p + 1, :], (8, 128))
        mult = {}
        lines, scaled, rows = [], [], []
        for p in range(0, 8, 2):
            d, o, e = a[p, p], a[p + 1, p], a[p + 1, p + 1]
            root = lax.rsqrt(d * e - o * o)
            inverse = root * root
            for k in range(p + 2, 8):
                mult[k, p] = (a[k, p] * e - a[k, p + 1] * o) * inverse
                mult[k, p + 1] = (a[k, p + 1] * d - a[k, p] * o) * inverse
            for k in range(p + 2, 8):
                for c in range(p + 2, k + 1):
                    a[k, c] = a[k, c] - (mult[k, p] * a[c, p] + mult[k, p + 1] * a[c, p + 1])
            for r in (p, p + 1):
                unit = (lane == 8 * q + r).astype(F32)
                line = jnp.broadcast_to(hold[q, 8, r : r + 1, :], (8, 128))
                line = jnp.where(inside(q), unit, line)
                for k in range(p):
                    line = line - mult[r, k] * lines[k]
                lines.append(line)
            low, high = lines[p], lines[p + 1]
            turned = high * d - low * o
            scaled.append((low * e - high * o) * inverse)
            scaled.append(turned * inverse)
            top = lax.rsqrt(d)
            rows.append(low * top)
            rows.append(turned * (top * root))
        tiles[q] = stack(rows)
        return block, mult, scaled

    def update_next(q, mult, scaled):
        rest = jnp.where(inside(q), 0.0, tiles[q + 1])
        cols = []
        for p in range(0, 8, 2):
            for r in (p, p + 1):
                col = column(q + 1, q, r)
                for k in range(p):
                    col = col - mult[r, k] * cols[k]
                cols.append(col)
            rest = rest - (cols[p] * scaled[p] + cols[p + 1] * scaled[p + 1])
        tiles[q + 1] = rest

    def substitute(mult, scaled):
        back = list(scaled)
        for p in range(5, -1, -1):
            for k in range(7, p + 1 - p % 2, -1):
                back[p] = back[p] - mult[k, p] * back[k]
        return back

    for q in range(0, count, 2):
        block0, mult0, scaled0 = panel_of(q)
        update_next(q, mult0, scaled0)
        if q + 2 < count:
            back0 = substitute(mult0, scaled0)
            other = jnp.where(inside(q), 0.0, tiles[q + 2])
            for c in range(8):
                other = other - column(q + 2, q, c) * back0[c]
            tiles[q + 2] = other
        block1, mult1, scaled1 = panel_of(q + 1)
        if q + 2 < count:
            update_next(q + 1, mult1, scaled1)
            back1 = substitute(mult1, scaled1)
            both = inside(q) | inside(q + 1)
            right = jnp.concatenate(
                [jnp.where(inside(q + 1), 0.0, stack(back0)), stack(back1)], axis=0
            )
            far = stacked(jnp.concatenate([block0, block1], axis=0), right, 0, 0)
            for r in range(q + 3, count):
                tiles[r] = jnp.where(both, 0.0, tiles[r]) - far[8 * r : 8 * r + 8, :]
    for q in range(count):
        tiles[q] = jnp.where(lane <= sub + 8 * q, tiles[q], 0.0)
    return tiles


def solve_kernel(pos, mine, theirs, out, full, inv, turn, hold):
    d = pos[0]
    y = d // (NZ * NC)
    z = lax.rem(d // NC, NZ)
    c = lax.rem(d, NC)
    base = (y * NC + c) * 64 + z
    first = c == 0
    lane = lanes(128, 128)
    row = lax.broadcasted_iota(jnp.int32, (128, 128), 0)
    left = lane < 64
    eye = (lane == row).astype(F32) * damping

    for j in range(NY):
        for k in range(j + 1):
            s = slice(128 * (k % 2), 128 * (k % 2) + 128)
            even = jnp.where(first, mine[j, s, :], theirs[j, s, :])
            odd = jnp.where(first, theirs[j, s, :], mine[j, s, :])
            if k < 2:
                block = jnp.where(left, even, pltpu.roll(odd, 64, 1))
            else:
                block = jnp.where(left, pltpu.roll(even, 64, 1), odd)
            if j == k:
                block = block + eye
            full[128 * k : 128 * k + 128, 128 * j : 128 * j + 128] = block
        for k in range(j + 1, NY):
            full[128 * k : 128 * k + 128, 128 * j : 128 * j + 128] = jnp.zeros((128, 128), F32)
        even = jnp.where(first, mine[j, 256:272, :], theirs[j, 256:272, :])
        odd = jnp.where(first, theirs[j, 256:272, :], mine[j, 256:272, :])
        turn[pl.ds(0, 16, stride=2), :] = jnp.where(left[:16], even, pltpu.roll(odd, 64, 1))
        turn[pl.ds(1, 16, stride=2), :] = jnp.where(left[:16], pltpu.roll(even, 64, 1), odd)
        turned = turn[...].T
        unit = (row + 128 * j == base + (lane - 32) * 16).astype(F32)
        right = jnp.where(lane < 32, turned, jnp.where(lane < 36, unit, 0.0))
        full[128 * j : 128 * j + 128, 512:640] = right
    def step(k, carry):
        at = pl.multiple_of(k * 128, 128)
        s = pl.ds(at, 128)
        tiles = inverse_factor([full[pl.ds(at + 8 * t, 8), s] for t in range(16)], hold)
        for t in range(16):
            inv[8 * t : 8 * t + 8, :] = tiles[t]

        for j in range(4):

            @pl.when(k == j)
            def _():
                s = slice(128 * j, 128 * j + 128)
                after = 128 * j + 128
                strip = stacked(inv[...], full[s, after:640], 1, 0)
                full[s, 512:640] = strip[:, 512 - after :]
                if j < 3:
                    turned = strip[:, : 512 - after].T
                    full[after:512, after:640] -= stacked(turned, strip, 1, 0)

        return carry

    lax.fori_loop(0, 4, step, 0)
    right = full[:, 512:640]
    out[...] = stacked(right.T[32:40, :], right, 1, 0)[0:4, 0:32]


def solve(pos, mine, theirs):
    return pl.pallas_call(
        solve_kernel,
        out_shape=shape(4, 32),
        in_specs=[SM] + [VM] * 2,
        out_specs=VM,
        scratch_shapes=[
            pltpu.VMEM((512, 640), F32),
            pltpu.VMEM((128, 128), F32),
            pltpu.VMEM((128, 128), F32),
            pltpu.VMEM((16, 9, 8, 128), F32),
        ],
        compiler_params=params(),
        name="solve",
    )(pos, mine, theirs)


def index(y, z, c):
    return (y * NZ + z) * NC + c


def exchange(value, groups):
    return lax.all_to_all(value, "dp", 0, 0, axis_index_groups=groups, tiled=True)


def swap(value, partner):
    pairs = [
        (index(*partner(y, z, c)), index(y, z, c))
        for y in range(NY)
        for z in range(NZ)
        for c in range(NC)
    ]
    return lax.ppermute(value, "dp", pairs)


def other_core(y, z, c):
    return y, z, 1 - c


def shards(tg, ta, qg, qa, of, inf, tlen, qlen):
    ys, zs, cs = range(NY), range(NZ), range(NC)
    line_groups = [[index(y, z, c) for z in zs] for y in ys for c in cs]
    y_groups = [[index(y, z, c) for y in ys] for z in zs for c in cs]
    pos = lax.axis_index("dp").astype(jnp.int32).reshape(1)
    parts = project(tg, ta, qg, qa, of, inf)
    parts = lax.all_to_all(parts, "mp", 0, 0, tiled=True)
    zcopies, own = sketch(tlen, qlen, parts)
    pair = jnp.concatenate([own, swap(own, other_core)], axis=0)
    line = exchange(zcopies, line_groups).reshape(NZ * 32, 128)
    near = jnp.concatenate([pair, swap(pair, lambda y, z, c: (y ^ 1, z, c))], axis=0)
    away = swap(near, lambda y, z, c: (NY - 1 - y, z, c))
    tiles = lax.all_to_all(tile(pos, line, near, away), "mp", 0, 0, tiled=True)
    panels = panel(exchange(add(tiles), line_groups))
    mine = exchange(panels, y_groups)
    return solve(pos, mine, swap(mine, other_core))


def solution(mesh):
    return jax.shard_map(
        shards,
        mesh=mesh,
        in_specs=(
            P("dp", None, "mp"),
            P("dp", None, "mp"),
            P("dp", None, "mp"),
            P("dp", None, "mp"),
            P(None, "mp"),
            P(None, "mp"),
            P("dp"),
            P("dp"),
        ),
        out_specs=P("dp", "mp"),
        check_vma=False,
    )
```

```python
import jax
import jax.numpy as jnp
from jax import lax
from jax.experimental import pallas as pl
from jax.experimental.pallas import tpu as pltpu
from jax.sharding import PartitionSpec as P

damping = 2.0
F32 = jnp.float32
HIGHEST = lax.Precision.HIGHEST
MB = 1024 * 1024

NY, NZ, NC = 4, 16, 2
VM = pl.BlockSpec(memory_space=pltpu.VMEM)
SM = pl.BlockSpec(memory_space=pltpu.SMEM)
ANY = pl.BlockSpec(memory_space=pl.ANY)


def params(limit=40 * MB):
    return pltpu.CompilerParams(vmem_limit_bytes=limit)


def shape(*sizes):
    return jax.ShapeDtypeStruct(sizes, F32)


def dot(a, b, ca, cb, precision=HIGHEST):
    return lax.dot_general(
        a, b, (((ca,), (cb,)), ((), ())), precision=precision, preferred_element_type=F32
    )


def lanes(*sizes):
    return lax.broadcasted_iota(jnp.int32, sizes, 1)


CHUNKS = 4


def project_kernel(tg, ta, qg, qa, of, inf, out, g, a, fo, fi, acc, packed, sem):
    copies = []

    def start(src, dst):
        copy = pltpu.make_async_copy(src, dst, sem.at[len(copies)])
        copy.start()
        copies.append(copy)

    start(inf.at[0:32], fi.at[32:64])
    start(inf.at[32:64], fi.at[96:128])
    start(ta, a.at[0:4])
    start(qa, a.at[4:5])
    start(of.at[0:32], fo.at[0:32])
    start(of.at[32:64], fo.at[64:96])
    width = g.shape[2] // CHUNKS
    for j in range(CHUNKS):
        s = slice(j * width, (j + 1) * width)
        start(tg.at[:, :, s], g.at[0:4, :, s])
        start(qg.at[:, :, s], g.at[4:5, :, s])
    for at in (0, 64):
        fi[at : at + 32, :] = jnp.zeros((32, fi.shape[1]), fi.dtype)
        fo[at + 32 : at + 64, :] = jnp.zeros((32, fo.shape[1]), fo.dtype)
    for copy in copies[:4]:
        copy.wait()
    acc[...] = dot(a[...].reshape(320, a.shape[2]), fi[...], 1, 1, None)
    copies[4].wait()
    copies[5].wait()
    for j in range(CHUNKS):
        copies[6 + 2 * j].wait()
        copies[7 + 2 * j].wait()
        s = slice(j * width, (j + 1) * width)
        acc[...] += dot(g[:, :, s].reshape(320, width), fo[:, s], 1, 1, None)
    for p in range(4):
        for low, high, to, n in ((0, 128, 0, 128), (256, 288, 128, 32)):
            one = acc[low : low + n, :]
            two = acc[high : high + n, :]
            one = pltpu.roll(one, (128 - 32 * p) % 128, 1) if p else one
            two = pltpu.roll(two, (64 - 32 * p) % 128, 1) if p != 2 else two
            packed[p, to : to + n, :] = jnp.where(lanes(n, 128) < 64, one, two)
        start(packed.at[p], out.at[p])
    for copy in copies[6 + 2 * CHUNKS :]:
        copy.wait()


def project(tg, ta, qg, qa, of, inf):
    kg, ka = tg.shape[2], ta.shape[2]
    return pl.pallas_call(
        project_kernel,
        out_shape=shape(4, 160, 128),
        in_specs=[ANY] * 6,
        out_specs=ANY,
        scratch_shapes=[
            pltpu.VMEM((5, 64, kg), jnp.bfloat16),
            pltpu.VMEM((5, 64, ka), jnp.bfloat16),
            pltpu.VMEM((128, kg), jnp.bfloat16),
            pltpu.VMEM((128, ka), jnp.bfloat16),
            pltpu.VMEM((320, 128), F32),
            pltpu.VMEM((4, 160, 128), F32),
            pltpu.SemaphoreType.DMA((10 + 2 * CHUNKS,)),
        ],
        compiler_params=params(56 * MB),
        name="project",
    )(tg, ta, qg, qa, of, inf)


def sketch_kernel(tlen, qlen, parts, zcopies, own, square, trains, sem):
    lane = lanes(8, 128)

    def fold(row, col):
        total = None
        for g in range(4):
            piece = square[row + 8 * g : row + 8 * g + 8, :]
            shift = (32 * g - col) % 128
            piece = pltpu.roll(piece, shift, 1) if shift else piece
            piece = jnp.where((lane >= 32 * g) & (lane < 32 * g + 32), piece, 0.0)
            total = piece if total is None else total + piece
        return total

    def emit(e, tile):
        own[8 * e : 8 * e + 8, :] = tile
        if e < 4:
            trains[8 * e : 8 * e + 8, :] = tile

    def outer(low, n, weight):
        s = slice(low, low + n)
        x = (parts[0, s, :] + parts[1, s, :]) + (parts[2, s, :] + parts[3, s, :])
        square[...] = dot(x * weight, x, 0, 0)

    token = lax.broadcasted_iota(jnp.int32, (64, 128), 0)
    left = lanes(64, 128) < 64
    for e in range(2):
        length = jnp.where(left, tlen[e], tlen[e + 2])
        weight = (token < length).astype(F32) / length.astype(F32)
        outer(64 * e, 64, weight)
        emit(e, fold(0, 32))
        emit(e + 2, fold(64, 96))
    copies = [
        pltpu.make_async_copy(trains, zcopies.at[t], sem.at[t]) for t in range(NZ)
    ]
    for copy in copies:
        copy.start()
    token = token[0:32] + jnp.where(left[0:32], 0, 32)
    outer(128, 32, (token < qlen[0]).astype(F32))
    emit(4, fold(0, 32) + fold(64, 96))
    for copy in copies:
        copy.wait()


def sketch(tlen, qlen, parts):
    return pl.pallas_call(
        sketch_kernel,
        out_shape=(shape(NZ, 32, 128), shape(40, 128)),
        in_specs=[SM] * 2 + [VM],
        out_specs=(ANY, VM),
        scratch_shapes=[
            pltpu.VMEM((128, 128), F32),
            pltpu.VMEM((32, 128), F32),
            pltpu.SemaphoreType.DMA((NZ,)),
        ],
        compiler_params=params(),
        name="sketch",
    )(tlen, qlen, parts)


def tile_kernel(pos, line, near, away, out, cols, held):
    y = pos[0] // (NZ * NC)
    c = lax.rem(pos[0], NC)
    for t, pairs in enumerate((near, near, away, away)):
        at = y if t < 2 else NY - 1 - y
        at = at if t % 2 == 0 else at + 1 - 2 * lax.rem(at, 2)
        for h in range(2):
            b = at * NC + lax.rem(c + h, NC)
            start = pl.multiple_of(b * 40, 8)
            row = 80 * (t % 2) + 40 * h
            cols[pl.ds(start, 40), :] = pairs[row : row + 40, :]
    total = None
    for s in range(8):
        rows = [line[pl.ds(8 * i + s, NZ, stride=32), :] for i in range(4)]
        part = dot(cols[pl.ds(s, 40, stride=8), :], jnp.concatenate(rows, axis=0), 1, 1)
        total = part if total is None else total + part
    held[:, 0:64] = total
    held[:, 64:128] = total
    for p in range(4):
        out[p, 16:24, :] = jnp.zeros((8, 128), F32)
        for h in range(2):
            s = slice(64 * h, 64 * h + 64)
            for g in range(4):
                row = 5 * (4 * h + g)
                out[p, 4 * g : 4 * g + 4, s] = held[row : row + 4, s]
            row = 5 * (2 * p + h) + 4
            out[p, 16:17, s] = held[row : row + 1, s]


def tile(pos, line, near, away):
    return pl.pallas_call(
        tile_kernel,
        out_shape=shape(4, 24, 128),
        in_specs=[SM] + [VM] * 3,
        out_specs=VM,
        scratch_shapes=[pltpu.VMEM((320, 128), F32), pltpu.VMEM((40, 128), F32)],
        compiler_params=params(),
        name="tile",
    )(pos, line, near, away)


def add_kernel(parts, out):
    total = (parts[0] + parts[1]) + (parts[2] + parts[3])
    for t in range(NZ):
        out[t] = total


def add(parts):
    return pl.pallas_call(
        add_kernel,
        out_shape=shape(NZ, 24, 128),
        in_specs=[VM],
        out_specs=VM,
        compiler_params=params(),
        name="add",
    )(parts)


def panel_kernel(parts, out):
    for z in range(NZ):
        both = parts[z, 0:16, :]
        query = parts[z, 16:17, :]
        for t in range(NY):
            out[t, pl.ds(z, 16, stride=NZ), :] = both
            out[t, 256 + z : 257 + z, :] = query


def panel(parts):
    return pl.pallas_call(
        panel_kernel,
        out_shape=shape(NY, 272, 128),
        in_specs=[VM],
        out_specs=VM,
        compiler_params=params(),
        name="panel",
    )(parts)


def thirds(x):
    one = x.astype(jnp.bfloat16)
    x = x - one.astype(F32)
    two = x.astype(jnp.bfloat16)
    return one, two, (x - two.astype(F32)).astype(jnp.bfloat16)


def stacked(a, b, ca, cb):
    a1, a2, a3 = thirds(a)
    b1, b2, b3 = thirds(b)
    left = jnp.concatenate([a1, a1, a2, a2, a1, a3], axis=ca)
    right = jnp.concatenate([b1, b2, b1, b2, b3, b1], axis=cb)
    return dot(left, right, ca, cb, None)


def inverse_factor(tiles, hold):
    lane = lanes(8, 128)
    sub = lax.broadcasted_iota(jnp.int32, (8, 128), 0)
    count = len(tiles)
    tiles = list(tiles)

    def inside(q):
        return (lane >= 8 * q) & (lane < 8 * q + 8)

    def column(r, q, c):
        return jnp.broadcast_to(tiles[r][:, 8 * q + c : 8 * q + c + 1], (8, 128))

    def stack(rows):
        merged = rows[0]
        for p in range(1, 8):
            merged = jnp.where(sub == p, rows[p], merged)
        return merged

    def panel_of(q):
        block = tiles[q]
        hold[q, 8] = block
        a = {}
        for c in range(8):
            hold[q, c] = column(q, q, c)
            for p in range(c, 8):
                a[p, c] = jnp.broadcast_to(hold[q, c, p : p + 1, :], (8, 128))
        mult = {}
        lines, scaled, rows = [], [], []
        for p in range(0, 8, 2):
            d, o, e = a[p, p], a[p + 1, p], a[p + 1, p + 1]
            root = lax.rsqrt(d * e - o * o)
            inverse = root * root
            for k in range(p + 2, 8):
                mult[k, p] = (a[k, p] * e - a[k, p + 1] * o) * inverse
                mult[k, p + 1] = (a[k, p + 1] * d - a[k, p] * o) * inverse
            for k in range(p + 2, 8):
                for c in range(p + 2, k + 1):
                    a[k, c] = a[k, c] - (mult[k, p] * a[c, p] + mult[k, p + 1] * a[c, p + 1])
            for r in (p, p + 1):
                unit = (lane == 8 * q + r).astype(F32)
                line = jnp.broadcast_to(hold[q, 8, r : r + 1, :], (8, 128))
                line = jnp.where(inside(q), unit, line)
                for k in range(p):
                    line = line - mult[r, k] * lines[k]
                lines.append(line)
            low, high = lines[p], lines[p + 1]
            turned = high * d - low * o
            scaled.append((low * e - high * o) * inverse)
            scaled.append(turned * inverse)
            top = lax.rsqrt(d)
            rows.append(low * top)
            rows.append(turned * (top * root))
        tiles[q] = stack(rows)
        return block, mult, scaled

    def update_next(q, mult, scaled):
        rest = jnp.where(inside(q), 0.0, tiles[q + 1])
        cols = []
        for p in range(0, 8, 2):
            for r in (p, p + 1):
                col = column(q + 1, q, r)
                for k in range(p):
                    col = col - mult[r, k] * cols[k]
                cols.append(col)
            rest = rest - (cols[p] * scaled[p] + cols[p + 1] * scaled[p + 1])
        tiles[q + 1] = rest

    def substitute(mult, scaled):
        back = list(scaled)
        for p in range(5, -1, -1):
            for k in range(7, p + 1 - p % 2, -1):
                back[p] = back[p] - mult[k, p] * back[k]
        return back

    for q in range(0, count, 2):
        block0, mult0, scaled0 = panel_of(q)
        update_next(q, mult0, scaled0)
        if q + 2 < count:
            back0 = substitute(mult0, scaled0)
            other = jnp.where(inside(q), 0.0, tiles[q + 2])
            for c in range(8):
                other = other - column(q + 2, q, c) * back0[c]
            tiles[q + 2] = other
        block1, mult1, scaled1 = panel_of(q + 1)
        if q + 2 < count:
            update_next(q + 1, mult1, scaled1)
            back1 = substitute(mult1, scaled1)
            both = inside(q) | inside(q + 1)
            right = jnp.concatenate(
                [jnp.where(inside(q + 1), 0.0, stack(back0)), stack(back1)], axis=0
            )
            far = stacked(jnp.concatenate([block0, block1], axis=0), right, 0, 0)
            for r in range(q + 3, count):
                tiles[r] = jnp.where(both, 0.0, tiles[r]) - far[8 * r : 8 * r + 8, :]
    for q in range(count):
        tiles[q] = jnp.where(lane <= sub + 8 * q, tiles[q], 0.0)
    return tiles


def solve_kernel(pos, mine, theirs, out, full, inv, turn, hold):
    d = pos[0]
    y = d // (NZ * NC)
    z = lax.rem(d // NC, NZ)
    c = lax.rem(d, NC)
    base = (y * NC + c) * 64 + z
    first = c == 0
    lane = lanes(128, 128)
    row = lax.broadcasted_iota(jnp.int32, (128, 128), 0)
    left = lane < 64
    eye = (lane == row).astype(F32) * damping

    for j in range(NY):
        for k in range(j + 1):
            s = slice(128 * (k % 2), 128 * (k % 2) + 128)
            even = jnp.where(first, mine[j, s, :], theirs[j, s, :])
            odd = jnp.where(first, theirs[j, s, :], mine[j, s, :])
            if k < 2:
                block = jnp.where(left, even, pltpu.roll(odd, 64, 1))
            else:
                block = jnp.where(left, pltpu.roll(even, 64, 1), odd)
            if j == k:
                block = block + eye
            full[128 * k : 128 * k + 128, 128 * j : 128 * j + 128] = block
        for k in range(j + 1, NY):
            full[128 * k : 128 * k + 128, 128 * j : 128 * j + 128] = jnp.zeros((128, 128), F32)
        even = jnp.where(first, mine[j, 256:272, :], theirs[j, 256:272, :])
        odd = jnp.where(first, theirs[j, 256:272, :], mine[j, 256:272, :])
        turn[pl.ds(0, 16, stride=2), :] = jnp.where(left[:16], even, pltpu.roll(odd, 64, 1))
        turn[pl.ds(1, 16, stride=2), :] = jnp.where(left[:16], pltpu.roll(even, 64, 1), odd)
        turned = turn[...].T
        unit = (row + 128 * j == base + (lane - 32) * 16).astype(F32)
        right = jnp.where(lane < 32, turned, jnp.where(lane < 36, unit, 0.0))
        full[128 * j : 128 * j + 128, 512:640] = right
    def step(k, carry):
        at = pl.multiple_of(k * 128, 128)
        s = pl.ds(at, 128)
        tiles = inverse_factor([full[pl.ds(at + 8 * t, 8), s] for t in range(16)], hold)
        for t in range(16):
            inv[8 * t : 8 * t + 8, :] = tiles[t]

        for j in range(4):

            @pl.when(k == j)
            def _():
                s = slice(128 * j, 128 * j + 128)
                after = 128 * j + 128
                strip = stacked(inv[...], full[s, after:640], 1, 0)
                full[s, 512:640] = strip[:, 512 - after :]
                if j < 3:
                    turned = strip[:, : 512 - after].T
                    full[after:512, after:640] -= stacked(turned, strip, 1, 0)

        return carry

    lax.fori_loop(0, 4, step, 0)
    right = full[:, 512:640]
    for i in range(4):
        one = jnp.sum(right * right[:, 32 + i : 33 + i], axis=0, keepdims=True)
        out[i : i + 1, :] = one[:, 0:32]


def solve(pos, mine, theirs):
    return pl.pallas_call(
        solve_kernel,
        out_shape=shape(4, 32),
        in_specs=[SM] + [VM] * 2,
        out_specs=VM,
        scratch_shapes=[
            pltpu.VMEM((512, 640), F32),
            pltpu.VMEM((128, 128), F32),
            pltpu.VMEM((128, 128), F32),
            pltpu.VMEM((16, 9, 8, 128), F32),
        ],
        compiler_params=params(),
        name="solve",
    )(pos, mine, theirs)


def index(y, z, c):
    return (y * NZ + z) * NC + c


def exchange(value, groups):
    return lax.all_to_all(value, "dp", 0, 0, axis_index_groups=groups, tiled=True)


def swap(value, partner):
    pairs = [
        (index(*partner(y, z, c)), index(y, z, c))
        for y in range(NY)
        for z in range(NZ)
        for c in range(NC)
    ]
    return lax.ppermute(value, "dp", pairs)


def other_core(y, z, c):
    return y, z, 1 - c


def shards(tg, ta, qg, qa, of, inf, tlen, qlen):
    ys, zs, cs = range(NY), range(NZ), range(NC)
    line_groups = [[index(y, z, c) for z in zs] for y in ys for c in cs]
    y_groups = [[index(y, z, c) for y in ys] for z in zs for c in cs]
    pos = lax.axis_index("dp").astype(jnp.int32).reshape(1)
    parts = project(tg, ta, qg, qa, of, inf)
    parts = lax.all_to_all(parts, "mp", 0, 0, tiled=True)
    zcopies, own = sketch(tlen, qlen, parts)
    pair = jnp.concatenate([own, swap(own, other_core)], axis=0)
    line = exchange(zcopies, line_groups).reshape(NZ * 32, 128)
    near = jnp.concatenate([pair, swap(pair, lambda y, z, c: (y ^ 1, z, c))], axis=0)
    away = swap(near, lambda y, z, c: (NY - 1 - y, z, c))
    tiles = lax.all_to_all(tile(pos, line, near, away), "mp", 0, 0, tiled=True)
    panels = panel(exchange(add(tiles), line_groups))
    mine = exchange(panels, y_groups)
    return solve(pos, mine, swap(mine, other_core))


def solution(mesh):
    return jax.shard_map(
        shards,
        mesh=mesh,
        in_specs=(
            P("dp", None, "mp"),
            P("dp", None, "mp"),
            P("dp", None, "mp"),
            P("dp", None, "mp"),
            P(None, "mp"),
            P(None, "mp"),
            P("dp"),
            P("dp"),
        ),
        out_specs=P("dp", "mp"),
        check_vma=False,
    )
```

```python
import jax
import jax.numpy as jnp
from jax import lax
from jax.experimental import pallas as pl
from jax.experimental.pallas import tpu as pltpu
from jax.sharding import PartitionSpec as P

damping = 2.0
F32 = jnp.float32
HIGHEST = lax.Precision.HIGHEST
MB = 1024 * 1024

NY, NZ, NC = 4, 16, 2
VM = pl.BlockSpec(memory_space=pltpu.VMEM)
SM = pl.BlockSpec(memory_space=pltpu.SMEM)
ANY = pl.BlockSpec(memory_space=pl.ANY)


def params(limit=40 * MB):
    return pltpu.CompilerParams(vmem_limit_bytes=limit)


def shape(*sizes):
    return jax.ShapeDtypeStruct(sizes, F32)


def dot(a, b, ca, cb, precision=HIGHEST):
    return lax.dot_general(
        a, b, (((ca,), (cb,)), ((), ())), precision=precision, preferred_element_type=F32
    )


def lanes(*sizes):
    return lax.broadcasted_iota(jnp.int32, sizes, 1)


CHUNKS = 4


def project_kernel(tg, ta, qg, qa, of, inf, out, g, a, fo, fi, acc, sem):
    copies = []

    def start(src, dst):
        copy = pltpu.make_async_copy(src, dst, sem.at[len(copies)])
        copy.start()
        copies.append(copy)

    start(inf.at[0:32], fi.at[32:64])
    start(inf.at[32:64], fi.at[96:128])
    start(ta, a.at[0:4])
    start(qa, a.at[4:5])
    start(of.at[0:32], fo.at[0:32])
    start(of.at[32:64], fo.at[64:96])
    width = g.shape[2] // CHUNKS
    for j in range(CHUNKS):
        s = slice(j * width, (j + 1) * width)
        start(tg.at[:, :, s], g.at[0:4, :, s])
        start(qg.at[:, :, s], g.at[4:5, :, s])
    for at in (0, 64):
        fi[at : at + 32, :] = jnp.zeros((32, fi.shape[1]), fi.dtype)
        fo[at + 32 : at + 64, :] = jnp.zeros((32, fo.shape[1]), fo.dtype)
    for copy in copies[:4]:
        copy.wait()
    acc[...] = dot(a[...].reshape(320, a.shape[2]), fi[...], 1, 1, None)
    copies[4].wait()
    copies[5].wait()
    for j in range(CHUNKS):
        copies[6 + 2 * j].wait()
        copies[7 + 2 * j].wait()
        s = slice(j * width, (j + 1) * width)
        acc[...] += dot(g[:, :, s].reshape(320, width), fo[:, s], 1, 1, None)
    for low, high, to, n in ((0, 128, 0, 128), (256, 288, 128, 32)):
        left = lanes(n, 128) < 64
        first = acc[low : low + n, :]
        second = acc[high : high + n, :]
        for p in range(4):
            one = pltpu.roll(first, (128 - 32 * p) % 128, 1) if p else first
            two = pltpu.roll(second, (64 - 32 * p) % 128, 1) if p != 2 else second
            out[p, to : to + n, :] = jnp.where(left, one, two)


def project(tg, ta, qg, qa, of, inf):
    kg, ka = tg.shape[2], ta.shape[2]
    return pl.pallas_call(
        project_kernel,
        out_shape=shape(4, 160, 128),
        in_specs=[ANY] * 6,
        out_specs=VM,
        scratch_shapes=[
            pltpu.VMEM((5, 64, kg), jnp.bfloat16),
            pltpu.VMEM((5, 64, ka), jnp.bfloat16),
            pltpu.VMEM((128, kg), jnp.bfloat16),
            pltpu.VMEM((128, ka), jnp.bfloat16),
            pltpu.VMEM((320, 128), F32),
            pltpu.SemaphoreType.DMA((6 + 2 * CHUNKS,)),
        ],
        compiler_params=params(56 * MB),
        name="project",
    )(tg, ta, qg, qa, of, inf)


def sketch_kernel(tlen, qlen, parts, own, square):
    lane = lanes(8, 128)

    def fold(row, col):
        total = None
        for g in range(4):
            piece = square[row + 8 * g : row + 8 * g + 8, :]
            shift = (32 * g - col) % 128
            piece = pltpu.roll(piece, shift, 1) if shift else piece
            piece = jnp.where((lane >= 32 * g) & (lane < 32 * g + 32), piece, 0.0)
            total = piece if total is None else total + piece
        return total

    def emit(e, tile):
        own[8 * e : 8 * e + 8, :] = tile

    def outer(low, n, weight):
        s = slice(low, low + n)
        x = (parts[0, s, :] + parts[1, s, :]) + (parts[2, s, :] + parts[3, s, :])
        square[...] = dot(x * weight, x, 0, 0)

    token = lax.broadcasted_iota(jnp.int32, (64, 128), 0)
    left = lanes(64, 128) < 64
    for e in range(2):
        length = jnp.where(left, tlen[e], tlen[e + 2])
        weight = (token < length).astype(F32) / length.astype(F32)
        outer(64 * e, 64, weight)
        emit(e, fold(0, 32))
        emit(e + 2, fold(64, 96))
    token = token[0:32] + jnp.where(left[0:32], 0, 32)
    outer(128, 32, (token < qlen[0]).astype(F32))
    emit(4, fold(0, 32) + fold(64, 96))


def sketch(tlen, qlen, parts):
    return pl.pallas_call(
        sketch_kernel,
        out_shape=shape(40, 128),
        in_specs=[SM] * 2 + [VM],
        out_specs=VM,
        scratch_shapes=[pltpu.VMEM((128, 128), F32)],
        compiler_params=params(),
        name="sketch",
    )(tlen, qlen, parts)


def tile_kernel(pos, line, near, away, out, cols, held):
    y = pos[0] // (NZ * NC)
    c = lax.rem(pos[0], NC)
    for t, pairs in enumerate((near, near, away, away)):
        at = y if t < 2 else NY - 1 - y
        at = at if t % 2 == 0 else at + 1 - 2 * lax.rem(at, 2)
        for h in range(2):
            b = at * NC + lax.rem(c + h, NC)
            start = pl.multiple_of(b * 40, 8)
            row = 80 * (t % 2) + 40 * h
            cols[pl.ds(start, 40), :] = pairs[row : row + 40, :]
    total = None
    for s in range(8):
        rows = [line[pl.ds(8 * i + s, NZ, stride=32), :] for i in range(4)]
        part = dot(cols[pl.ds(s, 40, stride=8), :], jnp.concatenate(rows, axis=0), 1, 1)
        total = part if total is None else total + part
    held[:, 0:64] = total
    held[:, 64:128] = total
    for p in range(4):
        out[p, 16:24, :] = jnp.zeros((8, 128), F32)
        for h in range(2):
            s = slice(64 * h, 64 * h + 64)
            for g in range(4):
                row = 5 * (4 * h + g)
                out[p, 4 * g : 4 * g + 4, s] = held[row : row + 4, s]
            row = 5 * (2 * p + h) + 4
            out[p, 16:17, s] = held[row : row + 1, s]


def tile(pos, line, near, away):
    return pl.pallas_call(
        tile_kernel,
        out_shape=shape(4, 24, 128),
        in_specs=[SM] + [VM] * 3,
        out_specs=VM,
        scratch_shapes=[pltpu.VMEM((320, 128), F32), pltpu.VMEM((40, 128), F32)],
        compiler_params=params(),
        name="tile",
    )(pos, line, near, away)


def add_kernel(parts, out):
    total = (parts[0] + parts[1]) + (parts[2] + parts[3])
    for t in range(NZ):
        out[t] = total


def add(parts):
    return pl.pallas_call(
        add_kernel,
        out_shape=shape(NZ, 24, 128),
        in_specs=[VM],
        out_specs=VM,
        compiler_params=params(),
        name="add",
    )(parts)


def panel_kernel(parts, out):
    for z in range(NZ):
        both = parts[z, 0:16, :]
        query = parts[z, 16:17, :]
        for t in range(NY):
            out[t, pl.ds(z, 16, stride=NZ), :] = both
            out[t, 256 + z : 257 + z, :] = query


def panel(parts):
    return pl.pallas_call(
        panel_kernel,
        out_shape=shape(NY, 272, 128),
        in_specs=[VM],
        out_specs=VM,
        compiler_params=params(),
        name="panel",
    )(parts)


def thirds(x):
    one = x.astype(jnp.bfloat16)
    x = x - one.astype(F32)
    two = x.astype(jnp.bfloat16)
    return one, two, (x - two.astype(F32)).astype(jnp.bfloat16)


def stacked(a, b, ca, cb):
    a1, a2, a3 = thirds(a)
    b1, b2, b3 = thirds(b)
    left = jnp.concatenate([a1, a1, a2, a2, a1, a3], axis=ca)
    right = jnp.concatenate([b1, b2, b1, b2, b3, b1], axis=cb)
    return dot(left, right, ca, cb, None)


def inverse_factor(tiles, hold):
    lane = lanes(8, 128)
    sub = lax.broadcasted_iota(jnp.int32, (8, 128), 0)
    count = len(tiles)
    tiles = list(tiles)

    def inside(q):
        return (lane >= 8 * q) & (lane < 8 * q + 8)

    def column(r, q, c):
        return jnp.broadcast_to(tiles[r][:, 8 * q + c : 8 * q + c + 1], (8, 128))

    def stack(rows):
        merged = rows[0]
        for p in range(1, 8):
            merged = jnp.where(sub == p, rows[p], merged)
        return merged

    def panel_of(q):
        block = tiles[q]
        hold[q, 8] = block
        a = {}
        for c in range(8):
            hold[q, c] = column(q, q, c)
            for p in range(c, 8):
                a[p, c] = jnp.broadcast_to(hold[q, c, p : p + 1, :], (8, 128))
        mult = {}
        lines, scaled, rows = [], [], []
        for p in range(0, 8, 2):
            d, o, e = a[p, p], a[p + 1, p], a[p + 1, p + 1]
            root = lax.rsqrt(d * e - o * o)
            inverse = root * root
            for k in range(p + 2, 8):
                mult[k, p] = (a[k, p] * e - a[k, p + 1] * o) * inverse
                mult[k, p + 1] = (a[k, p + 1] * d - a[k, p] * o) * inverse
            for k in range(p + 2, 8):
                for c in range(p + 2, k + 1):
                    a[k, c] = a[k, c] - (mult[k, p] * a[c, p] + mult[k, p + 1] * a[c, p + 1])
            for r in (p, p + 1):
                unit = (lane == 8 * q + r).astype(F32)
                line = jnp.broadcast_to(hold[q, 8, r : r + 1, :], (8, 128))
                line = jnp.where(inside(q), unit, line)
                for k in range(p):
                    line = line - mult[r, k] * lines[k]
                lines.append(line)
            low, high = lines[p], lines[p + 1]
            turned = high * d - low * o
            scaled.append((low * e - high * o) * inverse)
            scaled.append(turned * inverse)
            top = lax.rsqrt(d)
            rows.append(low * top)
            rows.append(turned * (top * root))
        tiles[q] = stack(rows)
        return block, mult, scaled

    def update_next(q, mult, scaled):
        rest = jnp.where(inside(q), 0.0, tiles[q + 1])
        cols = []
        for p in range(0, 8, 2):
            for r in (p, p + 1):
                col = column(q + 1, q, r)
                for k in range(p):
                    col = col - mult[r, k] * cols[k]
                cols.append(col)
            rest = rest - (cols[p] * scaled[p] + cols[p + 1] * scaled[p + 1])
        tiles[q + 1] = rest

    def substitute(mult, scaled):
        back = list(scaled)
        for p in range(5, -1, -1):
            for k in range(7, p + 1 - p % 2, -1):
                back[p] = back[p] - mult[k, p] * back[k]
        return back

    for q in range(0, count, 2):
        block0, mult0, scaled0 = panel_of(q)
        update_next(q, mult0, scaled0)
        if q + 2 < count:
            back0 = substitute(mult0, scaled0)
            other = jnp.where(inside(q), 0.0, tiles[q + 2])
            for c in range(8):
                other = other - column(q + 2, q, c) * back0[c]
            tiles[q + 2] = other
        block1, mult1, scaled1 = panel_of(q + 1)
        if q + 2 < count:
            update_next(q + 1, mult1, scaled1)
            back1 = substitute(mult1, scaled1)
            both = inside(q) | inside(q + 1)
            right = jnp.concatenate(
                [jnp.where(inside(q + 1), 0.0, stack(back0)), stack(back1)], axis=0
            )
            far = stacked(jnp.concatenate([block0, block1], axis=0), right, 0, 0)
            for r in range(q + 3, count):
                tiles[r] = jnp.where(both, 0.0, tiles[r]) - far[8 * r : 8 * r + 8, :]
    for q in range(count):
        tiles[q] = jnp.where(lane <= sub + 8 * q, tiles[q], 0.0)
    return tiles


def solve_kernel(pos, mine, theirs, out, full, inv, turn, hold):
    d = pos[0]
    y = d // (NZ * NC)
    z = lax.rem(d // NC, NZ)
    c = lax.rem(d, NC)
    base = (y * NC + c) * 64 + z
    first = c == 0
    lane = lanes(128, 128)
    row = lax.broadcasted_iota(jnp.int32, (128, 128), 0)
    left = lane < 64
    eye = (lane == row).astype(F32) * damping

    for j in range(NY):
        for k in range(j + 1):
            s = slice(128 * (k % 2), 128 * (k % 2) + 128)
            even = jnp.where(first, mine[j, s, :], theirs[j, s, :])
            odd = jnp.where(first, theirs[j, s, :], mine[j, s, :])
            if k < 2:
                block = jnp.where(left, even, pltpu.roll(odd, 64, 1))
            else:
                block = jnp.where(left, pltpu.roll(even, 64, 1), odd)
            if j == k:
                block = block + eye
            full[128 * k : 128 * k + 128, 128 * j : 128 * j + 128] = block
        for k in range(j + 1, NY):
            full[128 * k : 128 * k + 128, 128 * j : 128 * j + 128] = jnp.zeros((128, 128), F32)
        even = jnp.where(first, mine[j, 256:272, :], theirs[j, 256:272, :])
        odd = jnp.where(first, theirs[j, 256:272, :], mine[j, 256:272, :])
        turn[pl.ds(0, 16, stride=2), :] = jnp.where(left[:16], even, pltpu.roll(odd, 64, 1))
        turn[pl.ds(1, 16, stride=2), :] = jnp.where(left[:16], pltpu.roll(even, 64, 1), odd)
        turned = turn[...].T
        unit = (row + 128 * j == base + (lane - 32) * 16).astype(F32)
        right = jnp.where(lane < 32, turned, jnp.where(lane < 36, unit, 0.0))
        full[128 * j : 128 * j + 128, 512:640] = right
    def step(k, carry):
        at = pl.multiple_of(k * 128, 128)
        s = pl.ds(at, 128)
        tiles = inverse_factor([full[pl.ds(at + 8 * t, 8), s] for t in range(16)], hold)
        for t in range(16):
            inv[8 * t : 8 * t + 8, :] = tiles[t]

        for j in range(4):

            @pl.when(k == j)
            def _():
                s = slice(128 * j, 128 * j + 128)
                after = 128 * j + 128
                strip = stacked(inv[...], full[s, after:640], 1, 0)
                full[s, 512:640] = strip[:, 512 - after :]
                if j < 3:
                    turned = strip[:, : 512 - after].T
                    full[after:512, after:640] -= stacked(turned, strip, 1, 0)

        return carry

    lax.fori_loop(0, 4, step, 0)
    right = full[:, 512:640]
    out[...] = stacked(right.T[32:40, :], right, 1, 0)[0:4, 0:32]


def solve(pos, mine, theirs):
    return pl.pallas_call(
        solve_kernel,
        out_shape=shape(4, 32),
        in_specs=[SM] + [VM] * 2,
        out_specs=VM,
        scratch_shapes=[
            pltpu.VMEM((512, 640), F32),
            pltpu.VMEM((128, 128), F32),
            pltpu.VMEM((128, 128), F32),
            pltpu.VMEM((16, 9, 8, 128), F32),
        ],
        compiler_params=params(),
        name="solve",
    )(pos, mine, theirs)


def index(y, z, c):
    return (y * NZ + z) * NC + c


def exchange(value, groups):
    return lax.all_to_all(value, "dp", 0, 0, axis_index_groups=groups, tiled=True)


def swap(value, partner):
    pairs = [
        (index(*partner(y, z, c)), index(y, z, c))
        for y in range(NY)
        for z in range(NZ)
        for c in range(NC)
    ]
    return lax.ppermute(value, "dp", pairs)


def other_core(y, z, c):
    return y, z, 1 - c


def shards(tg, ta, qg, qa, of, inf, tlen, qlen):
    ys, zs, cs = range(NY), range(NZ), range(NC)
    line_groups = [[index(y, z, c) for z in zs] for y in ys for c in cs]
    y_groups = [[index(y, z, c) for y in ys] for z in zs for c in cs]
    pos = lax.axis_index("dp").astype(jnp.int32).reshape(1)
    parts = project(tg, ta, qg, qa, of, inf)
    parts = lax.all_to_all(parts, "mp", 0, 0, tiled=True)
    own = sketch(tlen, qlen, parts)
    zcopies = jnp.broadcast_to(own[None, :32], (NZ, 32, 128))
    pair = jnp.concatenate([own, swap(own, other_core)], axis=0)
    line = exchange(zcopies, line_groups).reshape(NZ * 32, 128)
    near = jnp.concatenate([pair, swap(pair, lambda y, z, c: (y ^ 1, z, c))], axis=0)
    away = swap(near, lambda y, z, c: (NY - 1 - y, z, c))
    tiles = lax.all_to_all(tile(pos, line, near, away), "mp", 0, 0, tiled=True)
    panels = panel(exchange(add(tiles), line_groups))
    mine = exchange(panels, y_groups)
    return solve(pos, mine, swap(mine, other_core))


def solution(mesh):
    return jax.shard_map(
        shards,
        mesh=mesh,
        in_specs=(
            P("dp", None, "mp"),
            P("dp", None, "mp"),
            P("dp", None, "mp"),
            P("dp", None, "mp"),
            P(None, "mp"),
            P(None, "mp"),
            P("dp"),
            P("dp"),
        ),
        out_specs=P("dp", "mp"),
        check_vma=False,
    )
```
